256 devices in a mesh: band: 8 (over x, core), tile: 32 (over z, y).
Axes of the slice: x: 4, y: 4, z: 8, core: 2. Of those that a mesh axis runs over, the one named last changes fastest.
Arguments:
- mean_state: float32 [256, 4096], P('band', 'tile'), may hold values from -6 to 6
- modes: float32 [256, 256, 4096], P(None, 'band', 'tile'), may hold values from -6 to 6
- east_vel: float32 [256, 4096], P('band', 'tile'), may hold values from -0.4 to 0.4
- north_vel: float32 [256, 4096], P('band', 'tile'), may hold values from -0.4 to 0.4
- sea_mask: int32 [256, 4096], P('band', 'tile'), may hold values 0 or 1
- obs_index: int32 [8, 32, 64], P('band', 'tile'), may hold values from 0 to 4095
- obs_value: float32 [8, 32, 64], P('band', 'tile'), may hold values from -6 to 6
- obs_weight: float32 [8, 32, 64], P('band', 'tile'), may hold values from 0.02 to 0.2
Outputs:
- mean_analysis: float32 [256, 4096], P('band', 'tile')
- basis: float32 [256, 256, 4096], P(None, 'band', 'tile')
- root_factor: float32 [256, 256], replicated
The draws below stay inside these ranges and needn't reach their ends.
Inputs may be any that keep to these rules, and one draw needn't show every extreme that they name: `obs_index`: row-major index over the block's 32 x 128 points.
All inputs are finite; a program needn't handle non-finite values. No bound on the sum of `sea_mask` on one device may be relied on, other than what follows from the above.
Results may differ from the reference program's by a relative error of at most 0.000076.
Values sent between devices are 32-bit elements; how exact they have to be, the bound alone decides.
No kernel may reach another device: no remote copies, remote signals or barrier semaphores. Data moves between devices by JAX's collectives and lax.ppermute only.
A program may use at most 192 MiB of HBM per device.

```python
import math
import jax
import jax.numpy as jnp
from jax import lax

R = 256
LAT_DEV = 32
LON_DEV = 128
OBS_DEV = 64
BANDS = 8
TILES = 32
NLAT = 256
NLON = 4096


def plant(result, own_key, low, high):
    longest = result.shape.index(max(result.shape))
    spots = []
    for shift in (0, 1):
        where = [jax.random.randint(jax.random.fold_in(own_key, axis), (), 0, length) for axis, length in enumerate(result.shape)]
        where[longest] = (where[longest] + shift) % result.shape[longest]
        spots.append(tuple(where))
    return result.at[spots[0]].set(low).at[spots[1]].set(high)


def level_of(stream_key, dims, shards, smallest, high):
    def one(axis_at, parts):
        draws = jax.random.uniform(jax.random.fold_in(jax.random.fold_in(stream_key, 6), axis_at), (parts,), jnp.float32, smallest / len(shards), high / len(shards))
        return jnp.repeat(jnp.exp(draws), dims[axis_at] // parts).reshape((-1,) + (1,) * (len(dims) - axis_at - 1))

    gain = one(*shards[0])
    for cut in shards[1:]:
        gain = gain * one(*cut)
    return gain


def scatter_about(key, shape, width, most, split=(), kind=jnp.bfloat16):
    values = width * jax.random.normal(key, shape, jnp.float32)
    if split:
        values = values * level_of(key, shape, split, -0.22, 0.18)
    return jnp.clip(values, -most, most).astype(kind)


def setup_inputs(seed: int = 0) -> dict:
    streams_of = jax.random.split(jax.random.key(seed), 9)
    return {
        "mean_state": scatter_about(streams_of[0], (NLAT, NLON), 1.0, 6.0, ((0, 8), (1, 32)), jnp.float32),
        "modes": scatter_about(streams_of[1], (R, NLAT, NLON), 1.0, 6.0, ((1, 8), (2, 32)), jnp.float32),
        "east_vel": jnp.clip(jax.random.uniform(streams_of[2], (NLAT, NLON), jnp.float32, -0.4, 0.4) * level_of(streams_of[2], (NLAT, NLON), ((0, 8), (1, 32)), -0.4, 0.0), -0.4, 0.4),
        "north_vel": jnp.clip(jax.random.uniform(streams_of[3], (NLAT, NLON), jnp.float32, -0.4, 0.4) * level_of(streams_of[3], (NLAT, NLON), ((0, 8), (1, 32)), -0.4, 0.0), -0.4, 0.4),
        "sea_mask": plant((jax.random.randint(streams_of[4], (NLAT, NLON), 0, 10) < 9).astype(jnp.int32), jax.random.fold_in(streams_of[4], 1), 0, 1),
        "obs_index": plant(jax.random.randint(streams_of[5], (BANDS, TILES, OBS_DEV), 0, LAT_DEV * LON_DEV), jax.random.fold_in(streams_of[5], 1), 0, (LAT_DEV * LON_DEV) - 1).astype(jnp.int32),
        "obs_value": scatter_about(streams_of[6], (BANDS, TILES, OBS_DEV), 1.0, 6.0, ((0, 8), (1, 32)), jnp.float32),
        "obs_weight": jnp.clip(jnp.exp(math.log(0.2) - 2.3025851 * jax.random.uniform(streams_of[7], (BANDS, TILES, OBS_DEV), jnp.float32) ** level_of(streams_of[7], (BANDS, TILES, OBS_DEV), ((0, 8), (1, 32)), -0.2, 0.2)), 0.02, 0.2),
    }


HIGH = lax.Precision.HIGHEST

def advance(fields, east_vel, north_vel, sea_mask):
    padded = jnp.pad(fields, ((0, 0), (1, 1), (1, 1)))
    centre = padded[:, 1:-1, 1:-1]
    northern = padded[:, 2:, 1:-1]
    southern = padded[:, :-2, 1:-1]
    eastern = padded[:, 1:-1, 2:]
    western = padded[:, 1:-1, :-2]
    tendency = -0.5 * east_vel * (eastern - western) - 0.5 * north_vel * (northern - southern)
    tendency = tendency + 0.2 * (eastern + western + northern + southern - 4.0 * centre)
    return sea_mask.astype(jnp.float32) * (centre + tendency)

def reference(mean_state, modes, east_vel, north_vel, sea_mask, obs_index, obs_value, obs_weight):
    npts = NLAT * NLON
    mean_fore = advance(mean_state[None], east_vel, north_vel, sea_mask)[0]
    lmat = advance(modes, east_vel, north_vel, sea_mask).reshape(R, npts)
    gram = lax.dot_general(lmat.astype(jnp.float32), lmat.astype(jnp.float32), (((1,), (1,)), ((), ())), precision=HIGH, preferred_element_type=jnp.float32)
    lower = jnp.linalg.cholesky(gram)
    qrows = lax.linalg.triangular_solve(lower, lmat, left_side=True, lower=True)
    band_ids = jnp.arange(BANDS, dtype=jnp.int32)[:, None, None]
    tile_ids = jnp.arange(TILES, dtype=jnp.int32)[None, :, None]
    lat_ids = band_ids * LAT_DEV + obs_index // LON_DEV
    lon_ids = tile_ids * LON_DEV + obs_index % LON_DEV
    flat_ids = (lat_ids * NLON + lon_ids).reshape(-1).astype(jnp.int32)
    hq = jnp.take(qrows, flat_ids, axis=1)
    weights = obs_weight.reshape(-1)
    diff = obs_value.reshape(-1) - jnp.take(mean_fore.reshape(npts), flat_ids)
    cq = lax.dot_general((hq * weights).astype(jnp.float32), hq.astype(jnp.float32), (((1,), (1,)), ((), ())), precision=HIGH, preferred_element_type=jnp.float32)
    bq = jnp.dot(hq.astype(jnp.float32), (weights * diff).astype(jnp.float32), precision=HIGH, preferred_element_type=jnp.float32)
    inner = jnp.dot(jnp.dot(lower, cq, precision=HIGH), lower.T, precision=HIGH)
    amat = jnp.eye(R, dtype=jnp.float32) + inner / (R - 1.0)
    factor = jnp.linalg.cholesky(amat)
    rhs = jnp.dot(lower, bq, precision=HIGH)[:, None]
    half = lax.linalg.triangular_solve(factor, rhs, left_side=True, lower=True)
    solved = lax.linalg.triangular_solve(factor, half, left_side=True, lower=True, transpose_a=True)
    coef = jnp.dot(lower.T, solved[:, 0], precision=HIGH) / (R - 1.0)
    increment = jnp.dot(coef, qrows, precision=HIGH)
    mean_analysis = mean_fore + increment.reshape(NLAT, NLON)
    scale = jnp.sqrt(jnp.float32(npts))
    basis = (qrows * scale).reshape(R, NLAT, NLON)
    root_factor = lax.linalg.triangular_solve(factor, lower, left_side=True, lower=True).T / scale
    return (mean_analysis, basis, root_factor)
```

```python
import jax
import jax.numpy as jnp
from jax import lax
from jax.sharding import PartitionSpec as P

HIGH = lax.Precision.HIGHEST
AXES = ("band", "tile")


def neighbours(block, axis, dim):
    count = lax.axis_size(axis)
    forward = [(i, i + 1) for i in range(count - 1)]
    backward = [(target, source) for source, target in forward]
    last = block.shape[dim] - 1
    low = lax.ppermute(lax.slice_in_dim(block, last, last + 1, axis=dim), axis, forward)
    high = lax.ppermute(lax.slice_in_dim(block, 0, 1, axis=dim), axis, backward)
    return low, high


def inner_rows(first, second):
    return lax.dot_general(
        first, second, (((1,), (1,)), ((), ())), precision=HIGH, preferred_element_type=jnp.float32
    )


def sum_everywhere(rows):
    mine = lax.all_to_all(rows, AXES, 0, 0, tiled=False).sum(0)
    return lax.all_to_all(jnp.broadcast_to(mine[None], rows.shape), AXES, 0, 0, tiled=False)


def body(mean_state, modes, east_vel, north_vel, sea_mask, obs_index, obs_value, obs_weight):
    count, lat_rows, lon_cols = modes.shape
    points = lat_rows * lon_cols
    fields = jnp.concatenate([mean_state[None], modes], axis=0)
    south, north = neighbours(fields, "band", 1)
    west, east = neighbours(fields, "tile", 2)
    northern = jnp.concatenate([fields[:, 1:], north], axis=1)
    southern = jnp.concatenate([south, fields[:, :-1]], axis=1)
    eastern = jnp.concatenate([fields[:, :, 1:], east], axis=2)
    western = jnp.concatenate([west, fields[:, :, :-1]], axis=2)
    tendency = -0.5 * east_vel * (eastern - western) - 0.5 * north_vel * (northern - southern)
    tendency = tendency + 0.2 * (eastern + western + northern + southern - 4.0 * fields)
    advanced = sea_mask.astype(jnp.float32) * (fields + tendency)
    mean_fore = advanced[0].reshape(points)
    lmodes = advanced[1:].reshape(count, points)
    indices = obs_index.reshape(-1)
    weights = obs_weight.reshape(-1)
    diff = obs_value.reshape(-1) - jnp.take(mean_fore, indices)
    gram = inner_rows(lmodes, lmodes)
    lobs = jnp.take(lmodes, indices, axis=1)
    obs_c = inner_rows(lobs * weights, lobs)
    obs_b = jnp.dot(lobs, weights * diff, precision=HIGH, preferred_element_type=jnp.float32)
    both = jnp.tril(gram) + jnp.triu(obs_c, 1)
    tail = jnp.stack([jnp.diagonal(obs_c), obs_b], axis=1)
    tail = jnp.pad(tail, ((0, 0), (0, 126)))
    packed = jnp.concatenate([both, tail], axis=1).reshape(count, 3, 128)
    total = sum_everywhere(packed).reshape(count, 384)
    both = total[:, :256]
    diag_c, b_total = total[:, 256], total[:, 257]
    low = jnp.tril(both, -1)
    gram = low + low.T + jnp.diag(jnp.diagonal(both))
    up = jnp.triu(both, 1)
    c_total = up + up.T + jnp.diag(diag_c)
    identity = jnp.eye(count, dtype=jnp.float32)
    amat = identity + c_total / (count - 1.0)
    lower, factor = jnp.linalg.cholesky(jnp.stack([gram, amat]))
    total_points = points * lax.axis_size("band") * lax.axis_size("tile")
    scale = jnp.sqrt(jnp.float32(total_points))
    linv = lax.linalg.triangular_solve(lower, identity, left_side=True, lower=True)
    right = jnp.concatenate([lower, b_total[:, None]], axis=1)
    half = lax.linalg.triangular_solve(factor, right, left_side=True, lower=True)
    root_factor = half[:, :count].T / scale
    solved = lax.linalg.triangular_solve(
        factor, half[:, count:], left_side=True, lower=True, transpose_a=True
    )[:, 0]
    increment = jnp.dot(solved / (count - 1.0), lmodes, precision=HIGH)
    mean_analysis = (mean_fore + increment).reshape(lat_rows, lon_cols)
    basis = jnp.dot(linv * scale, lmodes, precision=HIGH).reshape(count, lat_rows, lon_cols)
    return (mean_analysis, basis, root_factor)


def solution(mesh):
    return jax.shard_map(
        body,
        mesh=mesh,
        in_specs=(
            P("band", "tile"),
            P(None, "band", "tile"),
            P("band", "tile"),
            P("band", "tile"),
            P("band", "tile"),
            P("band", "tile", None),
            P("band", "tile", None),
            P("band", "tile", None),
        ),
        out_specs=(P("band", "tile"), P(None, "band", "tile"), P()),
        check_vma=False,
    )
```

```python
import functools

import jax
import jax.numpy as jnp
from jax import lax
from jax.experimental import pallas as pl
from jax.experimental.pallas import tpu as pltpu
from jax.sharding import PartitionSpec as P

HIGH = lax.Precision.HIGHEST
PANEL = 16
LANES = 128
PACK = 576
VMEM = pl.BlockSpec(memory_space=pltpu.VMEM)
SMEM = pl.BlockSpec(memory_space=pltpu.SMEM)
ROOM = pltpu.CompilerParams(vmem_limit_bytes=48 * 2**20)


def high_dot(a, b, dims):
    return lax.dot_general(
        a, b, (dims, ((), ())), precision=HIGH, preferred_element_type=jnp.float32
    )


def lanes_of(shape):
    return lax.broadcasted_iota(jnp.int32, shape, len(shape) - 1)


def edges_kernel(groups, modes_ref, mean_ref, slab_ref, low_ref, high_ref, west_ref, east_ref):
    step = pl.program_id(0)
    rows, lats = modes_ref.shape[0], modes_ref.shape[1]
    total = rows * groups
    lane = lanes_of((rows, LANES))
    west = jnp.zeros((rows, LANES), jnp.float32)
    east = jnp.zeros((rows, LANES), jnp.float32)
    here = pl.ds(pl.multiple_of(step * rows, rows), rows)
    for lat in range(lats):
        slab = modes_ref[:, lat, :]
        slab_ref[lat] = slab
        turned = pltpu.roll(slab, lat + 1, 1)
        west = jnp.where(lane == lat + 1, turned, west)
        east = jnp.where(lane == lat, turned, east)
        if lat == 0:
            low_ref[here] = slab
        if lat == lats - 1:
            high_ref[here] = slab
    base = step * lats
    west = pltpu.roll(west, base, 1)
    east = pltpu.roll(east, base, 1)
    from_base = lanes_of((rows, LANES)) - base
    east_here = (from_base >= 0) & (from_base < lats)
    shifted = lax.rem(from_base + LANES - 1, LANES)
    west_here = (shifted >= 0) & (shifted < lats)
    east_ref[0:rows] = jnp.where(east_here, east, east_ref[0:rows])
    west_ref[0:rows] = jnp.where(west_here, west, west_ref[0:rows])

    @pl.when(step == 0)
    def _():
        west_ref[rows : rows + lats] = mean_ref[...]
        east_ref[rows : rows + lats] = mean_ref[...]
        low_ref[total : total + 8] = jnp.broadcast_to(mean_ref[0:1], (8, LANES))
        high_ref[total : total + 8] = jnp.broadcast_to(mean_ref[lats - 1 : lats], (8, LANES))


def edges_of(modes, mean_state):
    count, lats, lons = modes.shape
    groups = lons // lats
    rows = count // groups
    whole = lambda shape: pl.BlockSpec(shape, lambda i: (0,) * len(shape))
    sides = [(count + 8, lons), (count + 8, lons), (rows + lats, lons), (rows + lats, lons)]
    return pl.pallas_call(
        functools.partial(edges_kernel, groups),
        grid=(groups,),
        in_specs=[pl.BlockSpec((rows, lats, lons), lambda i: (i, 0, 0)), whole((lats, lons))],
        out_specs=[pl.BlockSpec((lats, rows, lons), lambda i: (0, i, 0))] + [whole(s) for s in sides],
        out_shape=[jax.ShapeDtypeStruct((lats, count, lons), jnp.float32)]
        + [jax.ShapeDtypeStruct(s, jnp.float32) for s in sides],
        compiler_params=ROOM,
        name="edges",
    )(modes, mean_state)


def split(value):
    top = value.astype(jnp.bfloat16)
    return top, (value - top.astype(jnp.float32)).astype(jnp.bfloat16)


def pair_rows(a, b):
    return lax.dot_general(a, b, (((1,), (1,)), ((), ())), preferred_element_type=jnp.float32)


def sums_kernel(
    slab_ref, mean_ref, north_ref, south_ref, east_ref, west_ref, uvel_ref, vvel_ref, mask_ref,
    index_ref, value_ref, weight_ref, adv_ref, fore_ref, pack_ref, coef, parts, seen, seen_mean,
):
    lats, count, lons = slab_ref.shape
    groups = lons // lats
    rows = count // groups
    sea = mask_ref[...].astype(jnp.float32)
    half_u, half_v = 0.5 * uvel_ref[...], 0.5 * vvel_ref[...]
    coef[0] = sea * 0.2
    coef[1] = sea * (0.2 - half_u)
    coef[2] = sea * (0.2 + half_u)
    coef[3] = sea * (0.2 - half_v)
    coef[4] = sea * (0.2 + half_v)
    first = lanes_of((lats, lons)) == 0
    last = lanes_of((lats, lons)) == lons - 1
    mean = mean_ref[...]
    eastern = jnp.where(last, east_ref[rows : rows + lats, 0:1], pltpu.roll(mean, lons - 1, 1))
    western = jnp.where(first, west_ref[rows : rows + lats, lons - 1 : lons], pltpu.roll(mean, 1, 1))
    northern = jnp.concatenate([mean[1:], north_ref[count : count + 1]], axis=0)
    southern = jnp.concatenate([south_ref[count : count + 1], mean[:-1]], axis=0)
    fore = coef[0] * mean + coef[1] * eastern + coef[2] * western
    fore_ref[...] = fore + coef[3] * northern + coef[4] * southern

    first = lanes_of((rows, lons)) == 0
    last = lanes_of((rows, lons)) == lons - 1

    def advance(lat, northern, southern):
        factors = [coef[i, pl.ds(lat, 1), :] for i in range(5)]
        out = []
        for g in range(groups):
            span = slice(g * rows, (g + 1) * rows)
            centre = slab_ref[lat, span, :]
            east_edge = pltpu.roll(east_ref[0:rows], lax.rem(3 * lons - 2 - g * lats - lat, lons), 1)
            west_edge = pltpu.roll(west_ref[0:rows], lax.rem(2 * lons - g * lats - lat, lons), 1)
            eastern = jnp.where(last, east_edge, pltpu.roll(centre, lons - 1, 1))
            western = jnp.where(first, west_edge, pltpu.roll(centre, 1, 1))
            moved = factors[0] * centre + factors[1] * eastern + factors[2] * western
            moved = moved + factors[3] * northern[span, :] + factors[4] * southern[span, :]
            adv_ref[lat, span, :] = moved
            out.append(moved)
        return jnp.concatenate(out, axis=0)

    def add(lat, one, two):
        top, low = split(jnp.concatenate([one, two], axis=1))
        parts[0] += pair_rows(top, top) + pair_rows(low, low)
        parts[1] += pair_rows(top, low)

    parts[...] = jnp.zeros_like(parts)
    add(0, advance(0, slab_ref.at[1], south_ref), advance(1, slab_ref.at[2], slab_ref.at[0]))

    def middle(i, carry):
        lat = 2 * i
        one = advance(lat, slab_ref.at[lat + 1], slab_ref.at[lat - 1])
        two = advance(lat + 1, slab_ref.at[lat + 2], slab_ref.at[lat])
        add(lat, one, two)
        return carry

    lax.fori_loop(1, lats // 2 - 1, middle, 0)
    end = lats - 1
    add(
        end - 1,
        advance(end - 1, slab_ref.at[end], slab_ref.at[end - 2]),
        advance(end, north_ref, slab_ref.at[end - 1]),
    )

    observed = index_ref.shape[-1]
    seen[...] = jnp.zeros_like(seen)
    seen_mean[...] = jnp.zeros_like(seen_mean)
    lane = lanes_of((count, lons))

    def look(k, carry):
        point = index_ref[0, 0, k]
        lat, lon = point // lons, lax.rem(point, lons)
        turn = lax.rem(k + lons - lon, lons)
        column = pltpu.roll(adv_ref[lat], turn, 1)
        seen[...] = jnp.where(lane == k, column, seen[...])
        line = pltpu.roll(jnp.broadcast_to(fore_ref[pl.ds(lat, 1), :], (8, lons)), turn, 1)
        seen_mean[...] = jnp.where(lane[0:8] == k, line, seen_mean[...])
        return carry

    lax.fori_loop(0, observed, look, 0)
    used = lanes_of((1, lons)) < observed
    weights = jnp.where(used, weight_ref[...], 0.0)
    diff = value_ref[...] - seen_mean[0:1]
    found = seen[...]
    obs_c = high_dot(found * weights, found, ((1,), (1,)))
    obs_b = high_dot(jnp.broadcast_to(weights * diff, (8, lons)), found, ((1,), (1,)))
    cross = parts[1]
    gram = parts[0] + (cross + cross.T)
    row = lax.broadcasted_iota(jnp.int32, (count, count), 0)
    col = lax.broadcasted_iota(jnp.int32, (count, count), 1)
    both = jnp.where(row >= col, gram, obs_c)
    diag_c = jnp.sum(jnp.where(row == col, obs_c, 0.0), axis=0, keepdims=True)
    pack_ref[0:count] = both[:, 0:lons]
    pack_ref[count : 2 * count] = both[:, lons:]
    pack_ref[2 * count :] = jnp.zeros((PACK - 2 * count, lons), jnp.float32)
    for i, line in enumerate((diag_c, obs_b[0:1])):
        pack_ref[2 * count + 2 * i : 2 * count + 2 * i + 1] = line[:, 0:lons]
        pack_ref[2 * count + 2 * i + 1 : 2 * count + 2 * i + 2] = line[:, lons:]


def sums_of(slabs, mean_state, sides, east_vel, north_vel, sea_mask, obs_index, obs_value, obs_weight):
    lats, count, lons = slabs.shape
    pad = lambda x: jnp.pad(x.reshape(1, -1), ((0, 0), (0, lons - x.size)))
    return pl.pallas_call(
        sums_kernel,
        in_specs=[VMEM] * 9 + [SMEM] + [VMEM] * 2,
        out_specs=[VMEM] * 3,
        out_shape=[
            jax.ShapeDtypeStruct((lats, count, lons), jnp.float32),
            jax.ShapeDtypeStruct((lats, lons), jnp.float32),
            jax.ShapeDtypeStruct((PACK, lons), jnp.float32),
        ],
        scratch_shapes=[
            pltpu.VMEM((5, lats, lons), jnp.float32),
            pltpu.VMEM((2, count, count), jnp.float32),
            pltpu.VMEM((count, lons), jnp.float32),
            pltpu.VMEM((8, lons), jnp.float32),
        ],
        compiler_params=ROOM,
        name="sums",
    )(slabs, mean_state, *sides, east_vel, north_vel, sea_mask, obs_index, pad(obs_value), pad(obs_weight))


def exchange(value, axis, mask):
    return lax.ppermute(value, axis, [(i, i ^ mask) for i in range(lax.axis_size(axis))])


HALVING = (("band", 1, (0,)), ("band", 2, (1, 2)), ("band", 6, (2,)))
DOUBLING = (("tile", 1), ("tile", 3), ("tile", 4), ("tile", 8), ("tile", 24))


def sum_everywhere(value):
    uppers = []
    for axis, mask, bits in HALVING:
        half = value.shape[0] // 2
        low, high = value[:half], value[half:]
        upper = sum(lax.axis_index(axis) >> bit for bit in bits) & 1 == 1
        uppers.append(upper)
        value = jnp.where(upper, high, low) + exchange(jnp.where(upper, low, high), axis, mask)
    for axis, mask in DOUBLING:
        value = value + exchange(value, axis, mask)
    for (axis, mask, _), upper in zip(HALVING[::-1], uppers[::-1]):
        other = exchange(value, axis, mask)
        value = jnp.concatenate([jnp.where(upper, other, value), jnp.where(upper, value, other)])
    return value


def factor_panels(work, upper, inverse):
    size = work.shape[1]
    tiles = size // LANES
    lane = lanes_of((PANEL, LANES))
    sub = lax.broadcasted_iota(jnp.int32, (PANEL, LANES), 0)
    lane_row = lanes_of((1, LANES))
    for first in range(0, size, PANEL):
        home, at = first // LANES, first % LANES
        inside = (lane >= at) & (lane < at + PANEL)
        state = []
        for m in range(2):
            rows = [work[m, first : first + PANEL, t * LANES : (t + 1) * LANES] for t in range(tiles)]
            cols = [
                jnp.broadcast_to(rows[home][:, at + k : at + k + 1], (PANEL, LANES))
                for k in range(PANEL)
            ]
            block = jnp.where(inside, rows[home], 0.0)
            rows[home] = jnp.where(inside, jnp.where(lane == sub + at, 1.0, 0.0), rows[home])
            state.append((rows + [block], cols))
        for j in range(0, PANEL, 2):
            pair = (sub == j) | (sub == j + 1)
            for m in range(2):
                rows, cols = state[m]
                c0, c1 = cols[j], cols[j + 1]
                a, b, d = c0[j : j + 1], c1[j : j + 1], c1[j + 1 : j + 2]
                rdet = 1.0 / (a * d - b * b)
                i00, i01, i11 = d * rdet, -b * rdet, a * rdet
                m0 = c0 * i00 + c1 * i01
                m1 = c0 * i01 + c1 * i11
                m0 = jnp.where(sub == j, -i00, jnp.where(sub == j + 1, -i01, m0))
                m1 = jnp.where(sub == j, -i01, jnp.where(sub == j + 1, -i11, m1))
                for k in range(j + 2, PANEL):
                    ck = cols[k]
                    cols[k] = jnp.where(pair, 0.0, ck) - m0 * ck[j : j + 1] - m1 * ck[j + 1 : j + 2]
                ra = lax.rsqrt(a)
                ra = ra * (1.5 - 0.5 * a * ra * ra)
                ratio = b * ra * ra
                rest = d - ratio * b
                rb = lax.rsqrt(rest)
                rb = rb * (1.5 - 0.5 * rest * rb * rb)
                for t in range(tiles + 1):
                    r0, r1 = rows[t][j : j + 1], rows[t][j + 1 : j + 2]
                    done = (r0 * ra, (r1 - ratio * r0) * rb)
                    rows[t] = jnp.where(pair, 0.0, rows[t]) - m0 * r0 - m1 * r1
                    if t == tiles:
                        extra = done
                    elif t == home:
                        mine = done
                    else:
                        target, other = (inverse, upper) if t < home else (upper, inverse)
                        span = slice(t * LANES, (t + 1) * LANES)
                        target[m, first + j : first + j + 1, span] = done[0]
                        target[m, first + j + 1 : first + j + 2, span] = done[1]
                        other[m, first + j : first + j + 2, span] = jnp.zeros((2, LANES), jnp.float32)
                span = slice(home * LANES, (home + 1) * LANES)
                for e in range(2):
                    row = slice(first + j + e, first + j + e + 1)
                    left = lane_row < at + PANEL
                    inverse[m, row, span] = jnp.where(left, mine[e], 0.0)
                    corner = jnp.where(lane_row >= at + j + e, extra[e], 0.0)
                    upper[m, row, span] = jnp.where(left, corner, mine[e])
        for m in range(2):
            panel = jnp.concatenate(state[m][0][:tiles], axis=1)
            blocks = [panel]
            if at:
                blocks.insert(0, jnp.zeros((at, size), jnp.float32))
            if at + PANEL < LANES:
                blocks.append(jnp.zeros((LANES - at - PANEL, size), jnp.float32))
            panel = jnp.concatenate(blocks, axis=0)
            for start, stop in ((first + PANEL, first + 2 * PANEL), (first + 2 * PANEL, size)):
                if start >= min(stop, size):
                    continue
                left = work[m, start:stop, home * LANES : (home + 1) * LANES]
                change = high_dot(left, panel, ((1,), (0,)))
                place = lanes_of(left.shape)
                for t in range(tiles):
                    span = slice(t * LANES, (t + 1) * LANES)
                    if t == home:
                        old = jnp.where((place >= at) & (place < at + PANEL), 0.0, left)
                    else:
                        old = work[m, start:stop, span]
                    work[m, start:stop, span] = old - change[:, span]


def factor_kernel(scale, pack_ref, linv_ref, coef_ref, root_ref, work, upper, inverse):
    size = linv_ref.shape[0]
    row = lax.broadcasted_iota(jnp.int32, (size, size), 0)
    col = lax.broadcasted_iota(jnp.int32, (size, size), 1)
    eye = row == col
    both = jnp.concatenate([pack_ref[0:size], pack_ref[size : 2 * size]], axis=1)
    turned = both.T
    line = lambda i: jnp.concatenate(
        [pack_ref[2 * size + i : 2 * size + i + 1], pack_ref[2 * size + i + 1 : 2 * size + i + 2]], axis=1
    )
    gram = jnp.where(row >= col, both, turned)
    obs_c = jnp.where(row < col, both, jnp.where(eye, line(0), turned))
    only = jnp.where(eye, both, 0.0)
    q_row = lax.rsqrt(jnp.sum(only, axis=0, keepdims=True))
    work[0] = gram * q_row * lax.rsqrt(jnp.sum(only, axis=1, keepdims=True))
    work[1] = jnp.where(eye, 1.0, 0.0) + obs_c / (size - 1.0)
    factor_panels(work, upper, inverse)
    linv_ref[...] = inverse[0] * (q_row * scale)
    finv = inverse[1]
    root_ref[...] = high_dot(upper[0] * ((1.0 / q_row) / scale), finv, ((1,), (1,)))
    half = high_dot(jnp.broadcast_to(line(2), (8, size)), finv, ((1,), (1,)))
    coef_ref[...] = high_dot(half, finv, ((1,), (0,))) / (size - 1.0)


def factor_all(pack, size, scale):
    full = jax.ShapeDtypeStruct((size, size), jnp.float32)
    return pl.pallas_call(
        functools.partial(factor_kernel, scale),
        in_specs=[VMEM],
        out_specs=[VMEM] * 3,
        out_shape=(full, jax.ShapeDtypeStruct((8, size), jnp.float32), full),
        scratch_shapes=[pltpu.VMEM((2, size, size), jnp.float32)] * 3,
        compiler_params=ROOM,
        name="factors",
    )(pack)


def apply_kernel(adv_ref, linv_ref, coef_ref, fore_ref, basis_ref, mean_ref):
    lats = adv_ref.shape[0]
    count = linv_ref.shape[0]
    left = jnp.concatenate([linv_ref[...], coef_ref[...]], axis=0)
    for lat in range(0, lats, 2):
        pair = jnp.concatenate([adv_ref[lat], adv_ref[lat + 1]], axis=1)
        out = high_dot(left, pair, ((1,), (0,)))
        for e in range(2):
            part = out[:, e * LANES : (e + 1) * LANES]
            basis_ref[:, lat + e, :] = part[0:count]
            mean_ref[lat + e : lat + e + 1] = fore_ref[lat + e : lat + e + 1] + part[count : count + 1]


def apply_all(advanced, linv, coef, fore):
    lats, count, lons = advanced.shape
    step = 8
    whole = lambda shape: pl.BlockSpec(shape, lambda i: (0,) * len(shape))
    return pl.pallas_call(
        apply_kernel,
        grid=(lats // step,),
        in_specs=[
            pl.BlockSpec((step, count, lons), lambda i: (i, 0, 0)),
            whole(linv.shape),
            whole(coef.shape),
            pl.BlockSpec((step, lons), lambda i: (i, 0)),
        ],
        out_specs=[
            pl.BlockSpec((count, step, lons), lambda i: (0, i, 0)),
            pl.BlockSpec((step, lons), lambda i: (i, 0)),
        ],
        out_shape=[
            jax.ShapeDtypeStruct((count, lats, lons), jnp.float32),
            jax.ShapeDtypeStruct((lats, lons), jnp.float32),
        ],
        compiler_params=ROOM,
        name="apply",
    )(advanced, linv, coef, fore)


def body(mean_state, modes, east_vel, north_vel, sea_mask, obs_index, obs_value, obs_weight):
    count, lat_rows, lon_cols = modes.shape
    slabs, low, high, west, east = edges_of(modes, mean_state)
    up = lambda axis: [(i, i + 1) for i in range(lax.axis_size(axis) - 1)]
    down = lambda axis: [(j, i) for i, j in up(axis)]
    from_north = lax.ppermute(low, "band", down("band"))
    from_south = lax.ppermute(high, "band", up("band"))
    from_east = lax.ppermute(west, "tile", down("tile"))
    from_west = lax.ppermute(east, "tile", up("tile"))
    sides = (from_north, from_south, from_east, from_west)
    advanced, fore, pack = sums_of(
        slabs, mean_state, sides, east_vel, north_vel, sea_mask, obs_index, obs_value, obs_weight
    )
    pack = sum_everywhere(pack)
    points = lat_rows * lon_cols * lax.axis_size("band") * lax.axis_size("tile")
    linv, coef, root_factor = factor_all(pack, count, float(points) ** 0.5)
    basis, mean_analysis = apply_all(advanced, linv, coef, fore)
    return (mean_analysis, basis, root_factor)


def solution(mesh):
    return jax.shard_map(
        body,
        mesh=mesh,
        in_specs=(
            P("band", "tile"),
            P(None, "band", "tile"),
            P("band", "tile"),
            P("band", "tile"),
            P("band", "tile"),
            P("band", "tile", None),
            P("band", "tile", None),
            P("band", "tile", None),
        ),
        out_specs=(P("band", "tile"), P(None, "band", "tile"), P()),
        check_vma=False,
    )
```

```python
import functools

import jax
import jax.numpy as jnp
from jax import lax
from jax.experimental import pallas as pl
from jax.experimental.pallas import tpu as pltpu
from jax.sharding import Mesh
from jax.sharding import PartitionSpec as P

HIGH = lax.Precision.HIGHEST
PANEL = 16
LANES = 128
PACK = 576
VMEM = pl.BlockSpec(memory_space=pltpu.VMEM)
HBM = pl.BlockSpec(memory_space=pltpu.HBM)


def room(mebibytes):
    return pltpu.CompilerParams(vmem_limit_bytes=mebibytes * 2**20)


def high_dot(a, b, dims):
    return lax.dot_general(
        a, b, (dims, ((), ())), precision=HIGH, preferred_element_type=jnp.float32
    )


def lanes_of(shape):
    return lax.broadcasted_iota(jnp.int32, shape, len(shape) - 1)


def by_latitude(block, first):
    count = block.shape[0]
    turned = [jnp.swapaxes(block[r : r + 8, first : first + 8, :], 0, 1) for r in range(0, count, 8)]
    return [jnp.concatenate([part[e] for part in turned], axis=0) for e in range(8)]


def reads_of(source, target, sems):
    rows = target.shape[1]
    copies = [
        pltpu.make_async_copy(source.at[pl.ds(i * rows, rows)], target.at[i], sems.at[i])
        for i in range(target.shape[0])
    ]
    for copy in copies:
        copy.start()
    return copies


def edges_kernel(modes_ref, mean_ref, low_ref, high_ref, west_ref, east_ref, block, in_sem, mean_sem):
    chunks, rows, lats, lons = block.shape
    groups = lons // lats
    total = chunks * rows
    packed = total // groups
    reads = reads_of(modes_ref, block, in_sem)
    means = [
        pltpu.make_async_copy(mean_ref, side.at[pl.ds(packed, lats)], mean_sem.at[i])
        for i, side in enumerate((west_ref, east_ref))
    ]
    for copy in means:
        copy.start()
    lane = lanes_of((rows, lons))
    for i in range(chunks):
        base = i * rows // packed * lats
        here = slice(i * rows % packed, i * rows % packed + rows)
        span = slice(i * rows, (i + 1) * rows)
        reads[i].wait()
        west = jnp.zeros((rows, lons), jnp.float32) if base == 0 else west_ref[here]
        east = jnp.zeros((rows, lons), jnp.float32) if base == 0 else east_ref[here]
        for first in range(0, lats, 8):
            for e, line in enumerate(by_latitude(block.at[i], first)):
                lat = first + e
                moved = pltpu.roll(line, (base + lat + 1) % lons, 1)
                west = jnp.where(lane == (base + lat + 1) % lons, moved, west)
                east = jnp.where(lane == base + lat, moved, east)
                if lat == 0:
                    low_ref[span] = line
                if lat == lats - 1:
                    high_ref[span] = line
        west_ref[here] = west
        east_ref[here] = east
    for copy in means:
        copy.wait()
    low_ref[total : total + 8] = jnp.broadcast_to(west_ref[packed : packed + 1], (8, lons))
    high_ref[total : total + 8] = jnp.broadcast_to(west_ref[packed + lats - 1 : packed + lats], (8, lons))


def edges_of(modes, mean_state):
    count, lats, lons = modes.shape
    packed = count * lats // lons
    chunks = 8
    sides = [(count + 8, lons), (count + 8, lons), (packed + lats, lons), (packed + lats, lons)]
    return pl.pallas_call(
        edges_kernel,
        in_specs=[HBM] * 2,
        out_specs=[VMEM] * 4,
        out_shape=[jax.ShapeDtypeStruct(s, jnp.float32) for s in sides],
        scratch_shapes=[
            pltpu.VMEM((chunks, count // chunks, lats, lons), jnp.float32),
            pltpu.SemaphoreType.DMA((chunks,)),
            pltpu.SemaphoreType.DMA((2,)),
        ],
        compiler_params=room(61),
        name="edges",
    )(modes, mean_state)


def split(value):
    top = value.astype(jnp.bfloat16)
    return top, (value - top.astype(jnp.float32)).astype(jnp.bfloat16)


def pair_rows(a, b):
    return lax.dot_general(a, b, (((1,), (1,)), ((), ())), preferred_element_type=jnp.float32)


def sums_kernel(
    modes_ref, mean_ref, north_ref, south_ref, east_ref, west_ref, uvel_ref, vvel_ref, mask_ref,
    index_ref, value_ref, weight_ref, adv_hbm, fore_ref, pack_ref, slab_ref, adv_ref, coef, parts, seen, out_sem,
):
    lats, count, lons = slab_ref.shape
    chunks = out_sem.shape[0]
    deep = lats // chunks
    writes = []
    for i in range(chunks):
        span = pl.ds(i * deep, deep)
        writes.append(pltpu.make_async_copy(adv_ref.at[span], adv_hbm.at[span], out_sem.at[i]))
    groups = lons // lats
    rows = count // groups
    for r in range(0, count, rows):
        for lat in range(0, lats, 8):
            for e, line in enumerate(by_latitude(modes_ref.at[r : r + rows], lat)):
                slab_ref[lat + e, r : r + rows, :] = line
    sea = mask_ref[...].astype(jnp.float32)
    half_u, half_v = 0.5 * uvel_ref[...], 0.5 * vvel_ref[...]
    coef[0] = sea * 0.2
    coef[1] = sea * (0.2 - half_u)
    coef[2] = sea * (0.2 + half_u)
    coef[3] = sea * (0.2 - half_v)
    coef[4] = sea * (0.2 + half_v)
    first = lanes_of((lats, lons)) == 0
    last = lanes_of((lats, lons)) == lons - 1
    mean = mean_ref[...]
    eastern = jnp.where(last, east_ref[rows : rows + lats, 0:1], pltpu.roll(mean, lons - 1, 1))
    western = jnp.where(first, west_ref[rows : rows + lats, lons - 1 : lons], pltpu.roll(mean, 1, 1))
    northern = jnp.concatenate([mean[1:], north_ref[count : count + 1]], axis=0)
    southern = jnp.concatenate([south_ref[count : count + 1], mean[:-1]], axis=0)
    fore = coef[0] * mean + coef[1] * eastern + coef[2] * western
    fore_ref[...] = fore + coef[3] * northern + coef[4] * southern

    first = lanes_of((rows, lons)) == 0
    last = lanes_of((rows, lons)) == lons - 1

    def advance(lat, northern, southern):
        factors = [coef[i, pl.ds(lat, 1), :] for i in range(5)]
        out = []
        for g in range(groups):
            span = slice(g * rows, (g + 1) * rows)
            centre = slab_ref[lat, span, :]
            east_edge = pltpu.roll(east_ref[0:rows], (lons - 2 - g * lats - lat) % lons, 1)
            west_edge = pltpu.roll(west_ref[0:rows], (-g * lats - lat) % lons, 1)
            eastern = jnp.where(last, east_edge, pltpu.roll(centre, lons - 1, 1))
            western = jnp.where(first, west_edge, pltpu.roll(centre, 1, 1))
            moved = factors[0] * centre + factors[1] * eastern + factors[2] * western
            moved = moved + factors[3] * northern[span, :] + factors[4] * southern[span, :]
            adv_ref[lat, span, :] = moved
            out.append(moved)
        return jnp.concatenate(out, axis=0)

    observed = index_ref.shape[-1]
    point = index_ref[...]
    square = (observed, observed)
    eye = lax.broadcasted_iota(jnp.int32, square, 0) == lanes_of(square)
    point_col = jnp.sum(jnp.where(eye, point.astype(jnp.float32), 0.0), axis=1, keepdims=True)
    away = point_col.astype(jnp.int32) - lanes_of((observed, 2 * lons))

    parts[...] = jnp.zeros_like(parts)
    seen[...] = jnp.zeros_like(seen)
    for lat in range(0, lats, 2):
        rows_of = lambda i: south_ref if i < 0 else north_ref if i == lats else slab_ref.at[i]
        pair = [advance(i, rows_of(i + 1), rows_of(i - 1)) for i in (lat, lat + 1)]
        top, low = split(jnp.concatenate(pair, axis=1))
        parts[0] += pair_rows(top, top) + pair_rows(low, low)
        parts[1] += pair_rows(top, low)
        pick = jnp.where(away == lat * lons, 1.0, 0.0).astype(jnp.bfloat16)
        seen[...] += pair_rows(top, pick) + pair_rows(low, pick)
        if (lat + 2) % deep == 0:
            writes[lat // deep].start()

    lon_pick = jnp.where(lax.rem(point_col.astype(jnp.int32), lons) == lanes_of((observed, lons)), 1.0, 0.0)
    fore_at = high_dot(fore_ref[...], lon_pick, ((1,), (1,)))
    lat_of = lax.broadcasted_iota(jnp.int32, (lats, observed), 0)
    fore_at = jnp.sum(jnp.where(lat_of == point // lons, fore_at, 0.0), axis=0, keepdims=True)
    weights = weight_ref[...]
    diff = value_ref[...] - fore_at
    found = seen[...]
    obs_c = high_dot(found * weights, found, ((1,), (1,)))
    obs_b = high_dot(jnp.broadcast_to(weights * diff, (8, observed)), found, ((1,), (1,)))
    cross = parts[1]
    gram = parts[0] + (cross + cross.T)
    row = lax.broadcasted_iota(jnp.int32, (count, count), 0)
    col = lax.broadcasted_iota(jnp.int32, (count, count), 1)
    both = jnp.where(row >= col, gram, obs_c)
    diag_c = jnp.sum(jnp.where(row == col, obs_c, 0.0), axis=0, keepdims=True)
    pack_ref[0:count] = both[:, 0:lons]
    pack_ref[count : 2 * count] = both[:, lons:]
    pack_ref[2 * count :] = jnp.zeros((PACK - 2 * count, lons), jnp.float32)
    for i, line in enumerate((diag_c, obs_b[0:1])):
        pack_ref[2 * count + 2 * i : 2 * count + 2 * i + 1] = line[:, 0:lons]
        pack_ref[2 * count + 2 * i + 1 : 2 * count + 2 * i + 2] = line[:, lons:]
    for copy in writes:
        copy.wait()


def sums_of(modes, mean_state, sides, east_vel, north_vel, sea_mask, obs_index, obs_value, obs_weight):
    count, lats, lons = modes.shape
    line = lambda x: x.reshape(1, -1)
    return pl.pallas_call(
        sums_kernel,
        in_specs=[VMEM] * 12,
        out_specs=[HBM] + [VMEM] * 2,
        out_shape=[
            jax.ShapeDtypeStruct((lats, count, lons), jnp.float32),
            jax.ShapeDtypeStruct((lats, lons), jnp.float32),
            jax.ShapeDtypeStruct((PACK, lons), jnp.float32),
        ],
        scratch_shapes=[
            pltpu.VMEM((lats, count, lons), jnp.float32),
            pltpu.VMEM((lats, count, lons), jnp.float32),
            pltpu.VMEM((5, lats, lons), jnp.float32),
            pltpu.VMEM((2, count, count), jnp.float32),
            pltpu.VMEM((count, obs_index.size), jnp.float32),
            pltpu.SemaphoreType.DMA((8,)),
        ],
        compiler_params=room(50),
        name="sums",
    )(modes, mean_state, *sides, east_vel, north_vel, sea_mask, line(obs_index), line(obs_value), line(obs_weight))


def swap(value, axis, first):
    lower = range(first, lax.axis_size(axis) - 1, 2)
    pairs = [(i, i + 1) for i in lower] + [(i + 1, i) for i in lower]
    return lax.ppermute(value, axis, pairs)


def scatter_sum(value, axes):
    count = lax.axis_size(axes)
    return lax.all_to_all(value.reshape(count, -1, LANES), axes, 0, 0).sum(0)


def gather(value, axes):
    return lax.all_to_all(jnp.broadcast_to(value[None], (lax.axis_size(axes),) + value.shape), axes, 0, 0)


def sum_everywhere(value):
    half = value.shape[0] // 2
    low, high = value[:half], value[half:]
    upper = lax.axis_index("core") == 1
    value = jnp.where(upper, high, low) + swap(jnp.where(upper, low, high), "core", 0)
    value = scatter_sum(value, ("x", "y"))
    value = gather(value, "z").sum(0)
    value = gather(value, ("x", "y")).reshape(half, LANES)
    other = swap(value, "core", 0)
    return jnp.concatenate([jnp.where(upper, other, value), jnp.where(upper, value, other)])


def factor_panels(work, upper, inverse):
    size = work.shape[1]
    tiles = size // LANES
    lane = lanes_of((PANEL, LANES))
    sub = lax.broadcasted_iota(jnp.int32, (PANEL, LANES), 0)
    lane_row = lanes_of((1, LANES))
    for first in range(0, size, PANEL):
        home, at = first // LANES, first % LANES
        inside = (lane >= at) & (lane < at + PANEL)
        state = []
        for m in range(2):
            rows = [work[m, first : first + PANEL, t * LANES : (t + 1) * LANES] for t in range(tiles)]
            cols = [
                jnp.broadcast_to(rows[home][:, at + k : at + k + 1], (PANEL, LANES))
                for k in range(PANEL)
            ]
            block = jnp.where(inside, rows[home], 0.0)
            rows[home] = jnp.where(inside, jnp.where(lane == sub + at, 1.0, 0.0), rows[home])
            state.append((rows + [block], cols))
        for j in range(0, PANEL, 2):
            pair = (sub == j) | (sub == j + 1)
            for m in range(2):
                rows, cols = state[m]
                c0, c1 = cols[j], cols[j + 1]
                a, b, d = c0[j : j + 1], c1[j : j + 1], c1[j + 1 : j + 2]
                rdet = 1.0 / (a * d - b * b)
                i00, i01, i11 = d * rdet, -b * rdet, a * rdet
                m0 = c0 * i00 + c1 * i01
                m1 = c0 * i01 + c1 * i11
                m0 = jnp.where(sub == j, -i00, jnp.where(sub == j + 1, -i01, m0))
                m1 = jnp.where(sub == j, -i01, jnp.where(sub == j + 1, -i11, m1))
                for k in range(j + 2, PANEL):
                    ck = cols[k]
                    cols[k] = jnp.where(pair, 0.0, ck) - m0 * ck[j : j + 1] - m1 * ck[j + 1 : j + 2]
                ra = lax.rsqrt(a)
                ra = ra * (1.5 - 0.5 * a * ra * ra)
                ratio = b * ra * ra
                rest = d - ratio * b
                rb = lax.rsqrt(rest)
                rb = rb * (1.5 - 0.5 * rest * rb * rb)
                for t in range(tiles + 1):
                    r0, r1 = rows[t][j : j + 1], rows[t][j + 1 : j + 2]
                    done = (r0 * ra, (r1 - ratio * r0) * rb)
                    rows[t] = jnp.where(pair, 0.0, rows[t]) - m0 * r0 - m1 * r1
                    if t == tiles:
                        extra = done
                    elif t == home:
                        mine = done
                    else:
                        target, other = (inverse, upper) if t < home else (upper, inverse)
                        span = slice(t * LANES, (t + 1) * LANES)
                        target[m, first + j : first + j + 1, span] = done[0]
                        target[m, first + j + 1 : first + j + 2, span] = done[1]
                        other[m, first + j : first + j + 2, span] = jnp.zeros((2, LANES), jnp.float32)
                span = slice(home * LANES, (home + 1) * LANES)
                for e in range(2):
                    row = slice(first + j + e, first + j + e + 1)
                    left = lane_row < at + PANEL
                    inverse[m, row, span] = jnp.where(left, mine[e], 0.0)
                    corner = jnp.where(lane_row >= at + j + e, extra[e], 0.0)
                    upper[m, row, span] = jnp.where(left, corner, mine[e])
        for m in range(2):
            panel = jnp.concatenate(state[m][0][:tiles], axis=1)
            blocks = [panel]
            if at:
                blocks.insert(0, jnp.zeros((at, size), jnp.float32))
            if at + PANEL < LANES:
                blocks.append(jnp.zeros((LANES - at - PANEL, size), jnp.float32))
            panel = jnp.concatenate(blocks, axis=0)
            for start, stop in ((first + PANEL, first + 2 * PANEL), (first + 2 * PANEL, size)):
                if start >= min(stop, size):
                    continue
                left = work[m, start:stop, home * LANES : (home + 1) * LANES]
                change = high_dot(left, panel, ((1,), (0,)))
                place = lanes_of(left.shape)
                for t in range(tiles):
                    span = slice(t * LANES, (t + 1) * LANES)
                    if t == home:
                        old = jnp.where((place >= at) & (place < at + PANEL), 0.0, left)
                    else:
                        old = work[m, start:stop, span]
                    work[m, start:stop, span] = old - change[:, span]


def finish_kernel(
    scale, pack_ref, adv_hbm, fore_ref, mean_ref, basis_hbm, root_hbm,
    work, upper, inverse, root, adv, basis, in_sem, out_sem, root_sem,
):
    lats, size, lons = adv.shape
    steps = in_sem.shape[0]
    deep = lats // steps
    reads, writes = [], []
    for i in range(steps):
        span = pl.ds(i * deep, deep)
        reads.append(pltpu.make_async_copy(adv_hbm.at[span], adv.at[span], in_sem.at[i]))
        writes.append(pltpu.make_async_copy(basis.at[i], basis_hbm.at[:, span, :], out_sem.at[i]))
        reads[i].start()
    row = lax.broadcasted_iota(jnp.int32, (size, size), 0)
    col = lax.broadcasted_iota(jnp.int32, (size, size), 1)
    eye = row == col
    both = jnp.concatenate([pack_ref[0:size], pack_ref[size : 2 * size]], axis=1)
    turned = both.T
    line = lambda i: jnp.concatenate(
        [pack_ref[2 * size + i : 2 * size + i + 1], pack_ref[2 * size + i + 1 : 2 * size + i + 2]], axis=1
    )
    gram = jnp.where(row >= col, both, turned)
    obs_c = jnp.where(row < col, both, jnp.where(eye, line(0), turned))
    only = jnp.where(eye, both, 0.0)
    q_row = lax.rsqrt(jnp.sum(only, axis=0, keepdims=True))
    work[0] = gram * q_row * lax.rsqrt(jnp.sum(only, axis=1, keepdims=True))
    work[1] = jnp.where(eye, 1.0, 0.0) + obs_c / (size - 1.0)
    factor_panels(work, upper, inverse)
    finv = inverse[1]
    half = high_dot(jnp.broadcast_to(line(2), (8, size)), finv, ((1,), (1,)))
    coef = high_dot(half, finv, ((1,), (0,))) / (size - 1.0)
    left = jnp.concatenate([inverse[0] * (q_row * scale), coef], axis=0)
    for i in range(steps):
        reads[i].wait()
        wide = jnp.concatenate([adv[i * deep + e] for e in range(deep)], axis=1)
        out = high_dot(left, wide, ((1,), (0,)))
        parts = [out[:, e * lons : (e + 1) * lons] for e in range(deep)]
        for r in range(0, size, 8):
            basis[i, r : r + 8] = jnp.swapaxes(jnp.stack([part[r : r + 8] for part in parts]), 0, 1)
        writes[i].start()
        for e, part in enumerate(parts):
            lat = i * deep + e
            mean_ref[lat : lat + 1] = fore_ref[lat : lat + 1] + part[size : size + 1]
    root[...] = high_dot(upper[0] * ((1.0 / q_row) / scale), finv, ((1,), (1,)))
    writes.append(pltpu.make_async_copy(root, root_hbm, root_sem))
    writes[-1].start()
    for copy in writes:
        copy.wait()


def finish(pack, advanced, fore, scale):
    lats, size, lons = advanced.shape
    steps = 4
    square = (size, size)
    return pl.pallas_call(
        functools.partial(finish_kernel, scale),
        in_specs=[VMEM, HBM, VMEM],
        out_specs=[VMEM, HBM, HBM],
        out_shape=[
            jax.ShapeDtypeStruct((lats, lons), jnp.float32),
            jax.ShapeDtypeStruct((size, lats, lons), jnp.float32),
            jax.ShapeDtypeStruct(square, jnp.float32),
        ],
        scratch_shapes=[pltpu.VMEM((2,) + square, jnp.float32)] * 3
        + [
            pltpu.VMEM(square, jnp.float32),
            pltpu.VMEM((lats, size, lons), jnp.float32),
            pltpu.VMEM((steps, size, lats // steps, lons), jnp.float32),
            pltpu.SemaphoreType.DMA((steps,)),
            pltpu.SemaphoreType.DMA((steps,)),
            pltpu.SemaphoreType.DMA,
        ],
        compiler_params=room(61),
        name="finish",
    )(pack, advanced, fore)


def body(mean_state, modes, east_vel, north_vel, sea_mask, obs_index, obs_value, obs_weight):
    count, lat_rows, lon_cols = modes.shape
    low, high, west, east = edges_of(modes, mean_state)
    band, tile = ("x", "core"), ("z", "y")
    sides = []
    for axis, first, last in ((band, low, high), (tile, west, east)):
        even = lax.axis_index(axis) % 2 == 0
        one = swap(jnp.where(even, last, first), axis, 0)
        two = swap(jnp.where(even, first, last), axis, 1)
        sides += [jnp.where(even, one, two), jnp.where(even, two, one)]
    advanced, fore, pack = sums_of(
        modes, mean_state, sides, east_vel, north_vel, sea_mask, obs_index, obs_value, obs_weight
    )
    pack = sum_everywhere(pack)
    points = lat_rows * lon_cols * lax.axis_size(band) * lax.axis_size(tile)
    mean_analysis, basis, root_factor = finish(pack, advanced, fore, float(points) ** 0.5)
    return (mean_analysis, basis, root_factor)


def solution(mesh):
    mesh = Mesh(mesh.devices.reshape(4, 2, 8, 4), ("x", "core", "z", "y"))
    band, tile = ("x", "core"), ("z", "y")
    grid, blocks = P(band, tile), P(None, band, tile)
    obs = P(band, tile, None)
    return jax.shard_map(
        body,
        mesh=mesh,
        in_specs=(grid, blocks, grid, grid, grid, obs, obs, obs),
        out_specs=(grid, blocks, P()),
        check_vma=False,
    )
```

```python
import functools

import jax
import jax.numpy as jnp
from jax import lax
from jax.experimental import pallas as pl
from jax.experimental.pallas import tpu as pltpu
from jax.sharding import Mesh
from jax.sharding import PartitionSpec as P

HIGH = lax.Precision.HIGHEST
PANEL = 16
LANES = 128
PACK = 576
VMEM = pl.BlockSpec(memory_space=pltpu.VMEM)
HBM = pl.BlockSpec(memory_space=pltpu.HBM)


def room(mebibytes):
    return pltpu.CompilerParams(vmem_limit_bytes=mebibytes * 2**20)


def high_dot(a, b, dims):
    return lax.dot_general(
        a, b, (dims, ((), ())), precision=HIGH, preferred_element_type=jnp.float32
    )


def lanes_of(shape):
    return lax.broadcasted_iota(jnp.int32, shape, len(shape) - 1)


def by_latitude(block, first):
    count = block.shape[0]
    turned = [jnp.swapaxes(block[r : r + 8, first : first + 8, :], 0, 1) for r in range(0, count, 8)]
    return [jnp.concatenate([part[e] for part in turned], axis=0) for e in range(8)]


def reads_of(source, target, sems):
    rows = target.shape[1]
    copies = [
        pltpu.make_async_copy(source.at[pl.ds(i * rows, rows)], target.at[i], sems.at[i])
        for i in range(target.shape[0])
    ]
    for copy in copies:
        copy.start()
    return copies


def odd_sides():
    return lax.axis_index("core") == 1, lax.axis_index("y") % 2 == 1


def edges_kernel(
    modes_ref, mean_ref, lat_one, lat_two, lon_one, lon_two,
    low_ref, high_ref, west_ref, east_ref, block, in_sem, mean_sem,
):
    chunks, rows, lats, lons = block.shape
    groups = lons // lats
    total = chunks * rows
    packed = total // groups
    reads = reads_of(modes_ref, block, in_sem)
    means = [
        pltpu.make_async_copy(mean_ref, side.at[pl.ds(packed, lats)], mean_sem.at[i])
        for i, side in enumerate((west_ref, east_ref))
    ]
    for copy in means:
        copy.start()
    lane = lanes_of((rows, lons))
    for i in range(chunks):
        base = i * rows // packed * lats
        here = slice(i * rows % packed, i * rows % packed + rows)
        span = slice(i * rows, (i + 1) * rows)
        reads[i].wait()
        west = jnp.zeros((rows, lons), jnp.float32) if base == 0 else west_ref[here]
        east = jnp.zeros((rows, lons), jnp.float32) if base == 0 else east_ref[here]
        for first in range(0, lats, 8):
            for e, line in enumerate(by_latitude(block.at[i], first)):
                lat = first + e
                moved = pltpu.roll(line, (base + lat + 1) % lons, 1)
                west = jnp.where(lane == (base + lat + 1) % lons, moved, west)
                east = jnp.where(lane == base + lat, moved, east)
                if lat == 0:
                    low_ref[span] = line
                if lat == lats - 1:
                    high_ref[span] = line
        west_ref[here] = west
        east_ref[here] = east
    for copy in means:
        copy.wait()
    low_ref[total : total + 8] = jnp.broadcast_to(west_ref[packed : packed + 1], (8, lons))
    high_ref[total : total + 8] = jnp.broadcast_to(west_ref[packed + lats - 1 : packed + lats], (8, lons))
    odd_lat, odd_lon = odd_sides()
    for odd, below, above, one, two in (
        (odd_lat, low_ref, high_ref, lat_one, lat_two),
        (odd_lon, west_ref, east_ref, lon_one, lon_two),
    ):
        one[...] = jnp.where(odd, below[...], above[...])
        two[...] = jnp.where(odd, above[...], below[...])


def edges_of(modes, mean_state):
    count, lats, lons = modes.shape
    packed = count * lats // lons
    chunks = 8
    sides = [(count + 8, lons), (count + 8, lons), (packed + lats, lons), (packed + lats, lons)]
    return pl.pallas_call(
        edges_kernel,
        in_specs=[HBM] * 2,
        out_specs=[VMEM] * 4,
        out_shape=[jax.ShapeDtypeStruct(s, jnp.float32) for s in sides],
        scratch_shapes=[pltpu.VMEM(s, jnp.float32) for s in sides]
        + [
            pltpu.VMEM((chunks, count // chunks, lats, lons), jnp.float32),
            pltpu.SemaphoreType.DMA((chunks,)),
            pltpu.SemaphoreType.DMA((2,)),
        ],
        compiler_params=room(50),
        name="edges",
    )(modes, mean_state)


def split(value):
    top = value.astype(jnp.bfloat16)
    return top, (value - top.astype(jnp.float32)).astype(jnp.bfloat16)


def pair_rows(a, b):
    return lax.dot_general(a, b, (((1,), (1,)), ((), ())), preferred_element_type=jnp.float32)


def sums_kernel(
    modes_hbm, mean_ref, lat_one, lat_two, lon_one, lon_two, uvel_ref, vvel_ref, mask_ref,
    index_ref, value_ref, weight_ref, adv_hbm, keep_ref, send_ref,
    block, slab_ref, adv_ref, north_ref, south_ref, east_ref, west_ref, pack_ref, coef, parts, seen,
    in_sem, out_sem,
):
    lats, count, lons = slab_ref.shape
    reads = reads_of(modes_hbm, block, in_sem)
    odd_lat, odd_lon = odd_sides()
    for odd, below, above, one, two in (
        (odd_lat, south_ref, north_ref, lat_one, lat_two),
        (odd_lon, west_ref, east_ref, lon_one, lon_two),
    ):
        above[...] = jnp.where(odd, two[...], one[...])
        below[...] = jnp.where(odd, one[...], two[...])
    chunks = out_sem.shape[0] - 1
    deep = lats // chunks
    writes = []
    for i in range(chunks):
        span = pl.ds(i * deep, deep)
        writes.append(pltpu.make_async_copy(adv_ref.at[span], adv_hbm.at[span], out_sem.at[i]))
    groups = lons // lats
    rows = count // groups
    sea = mask_ref[...].astype(jnp.float32)
    half_u, half_v = 0.5 * uvel_ref[...], 0.5 * vvel_ref[...]
    coef[0] = sea * 0.2
    coef[1] = sea * (0.2 - half_u)
    coef[2] = sea * (0.2 + half_u)
    coef[3] = sea * (0.2 - half_v)
    coef[4] = sea * (0.2 + half_v)
    first = lanes_of((lats, lons)) == 0
    last = lanes_of((lats, lons)) == lons - 1
    mean = mean_ref[...]
    eastern = jnp.where(last, east_ref[rows : rows + lats, 0:1], pltpu.roll(mean, lons - 1, 1))
    western = jnp.where(first, west_ref[rows : rows + lats, lons - 1 : lons], pltpu.roll(mean, 1, 1))
    northern = jnp.concatenate([mean[1:], north_ref[count : count + 1]], axis=0)
    southern = jnp.concatenate([south_ref[count : count + 1], mean[:-1]], axis=0)
    fore = coef[0] * mean + coef[1] * eastern + coef[2] * western
    fore_ref = adv_ref.at[lats, 0:lats]
    fore_ref[...] = fore + coef[3] * northern + coef[4] * southern
    writes.append(pltpu.make_async_copy(fore_ref, adv_hbm.at[lats, 0:lats], out_sem.at[chunks]))
    writes[-1].start()
    for i, copy in enumerate(reads):
        copy.wait()
        part = block.shape[1]
        for lat in range(0, lats, 8):
            for e, line in enumerate(by_latitude(block.at[i], lat)):
                slab_ref[lat + e, i * part : (i + 1) * part, :] = line

    first = lanes_of((rows, lons)) == 0
    last = lanes_of((rows, lons)) == lons - 1

    def advance(lat, northern, southern):
        factors = [coef[i, pl.ds(lat, 1), :] for i in range(5)]
        out = []
        for g in range(groups):
            span = slice(g * rows, (g + 1) * rows)
            centre = slab_ref[lat, span, :]
            east_edge = pltpu.roll(east_ref[0:rows], (lons - 2 - g * lats - lat) % lons, 1)
            west_edge = pltpu.roll(west_ref[0:rows], (-g * lats - lat) % lons, 1)
            eastern = jnp.where(last, east_edge, pltpu.roll(centre, lons - 1, 1))
            western = jnp.where(first, west_edge, pltpu.roll(centre, 1, 1))
            moved = factors[0] * centre + factors[1] * eastern + factors[2] * western
            moved = moved + factors[3] * northern[span, :] + factors[4] * southern[span, :]
            adv_ref[lat, span, :] = moved
            out.append(moved)
        return jnp.concatenate(out, axis=0)

    observed = index_ref.shape[-1]
    point = index_ref[...]
    square = (observed, observed)
    eye = lax.broadcasted_iota(jnp.int32, square, 0) == lanes_of(square)
    point_col = jnp.sum(jnp.where(eye, point.astype(jnp.float32), 0.0), axis=1, keepdims=True)
    away = point_col.astype(jnp.int32) - lanes_of((observed, 2 * lons))

    parts[...] = jnp.zeros_like(parts)
    seen[...] = jnp.zeros_like(seen)
    for lat in range(0, lats, 2):
        rows_of = lambda i: south_ref if i < 0 else north_ref if i == lats else slab_ref.at[i]
        pair = [advance(i, rows_of(i + 1), rows_of(i - 1)) for i in (lat, lat + 1)]
        top, low = split(jnp.concatenate(pair, axis=1))
        parts[0] += pair_rows(top, top) + pair_rows(low, low)
        parts[1] += pair_rows(top, low)
        pick = jnp.where(away == lat * lons, 1.0, 0.0).astype(jnp.bfloat16)
        seen[...] += pair_rows(top, pick) + pair_rows(low, pick)
        if (lat + 2) % deep == 0:
            writes[lat // deep].start()

    lon_pick = jnp.where(lax.rem(point_col.astype(jnp.int32), lons) == lanes_of((observed, lons)), 1.0, 0.0)
    fore_at = high_dot(fore_ref[...], lon_pick, ((1,), (1,)))
    lat_of = lax.broadcasted_iota(jnp.int32, (lats, observed), 0)
    fore_at = jnp.sum(jnp.where(lat_of == point // lons, fore_at, 0.0), axis=0, keepdims=True)
    weights = weight_ref[...]
    diff = value_ref[...] - fore_at
    found = seen[...]
    obs_c = high_dot(found * weights, found, ((1,), (1,)))
    obs_b = high_dot(jnp.broadcast_to(weights * diff, (8, observed)), found, ((1,), (1,)))
    cross = parts[1]
    gram = parts[0] + (cross + cross.T)
    row = lax.broadcasted_iota(jnp.int32, (count, count), 0)
    col = lax.broadcasted_iota(jnp.int32, (count, count), 1)
    both = jnp.where(row >= col, gram, obs_c)
    diag_c = jnp.sum(jnp.where(row == col, obs_c, 0.0), axis=0, keepdims=True)
    pack_ref[0:count] = both[:, 0:lons]
    pack_ref[count : 2 * count] = both[:, lons:]
    pack_ref[2 * count :] = jnp.zeros((PACK - 2 * count, lons), jnp.float32)
    for i, line in enumerate((diag_c, obs_b[0:1])):
        pack_ref[2 * count + 2 * i : 2 * count + 2 * i + 1] = line[:, 0:lons]
        pack_ref[2 * count + 2 * i + 1 : 2 * count + 2 * i + 2] = line[:, lons:]
    half = PACK // 2
    keep_ref[...] = jnp.where(odd_lat, pack_ref[half:], pack_ref[:half])
    send_ref[...] = jnp.where(odd_lat, pack_ref[:half], pack_ref[half:])
    for copy in writes:
        copy.wait()


def sums_of(modes, mean_state, sides, east_vel, north_vel, sea_mask, obs_index, obs_value, obs_weight):
    count, lats, lons = modes.shape
    line = lambda x: x.reshape(1, -1)
    return pl.pallas_call(
        sums_kernel,
        in_specs=[HBM] + [VMEM] * 11,
        out_specs=[HBM] + [VMEM] * 2,
        out_shape=[jax.ShapeDtypeStruct((lats + 1, count, lons), jnp.float32)]
        + [jax.ShapeDtypeStruct((PACK // 2, lons), jnp.float32)] * 2,
        scratch_shapes=[
            pltpu.VMEM((8, count // 8, lats, lons), jnp.float32),
            pltpu.VMEM((lats, count, lons), jnp.float32),
            pltpu.VMEM((lats + 1, count, lons), jnp.float32),
        ]
        + [pltpu.VMEM(side.shape, jnp.float32) for side in sides]
        + [
            pltpu.VMEM((PACK, lons), jnp.float32),
            pltpu.VMEM((5, lats, lons), jnp.float32),
            pltpu.VMEM((2, count, count), jnp.float32),
            pltpu.VMEM((count, obs_index.size), jnp.float32),
            pltpu.SemaphoreType.DMA((8,)),
            pltpu.SemaphoreType.DMA((9,)),
        ],
        compiler_params=room(50),
        name="sums",
    )(modes, mean_state, *sides, east_vel, north_vel, sea_mask, line(obs_index), line(obs_value), line(obs_weight))


def swap(value, axis, first):
    lower = range(first, lax.axis_size(axis) - 1, 2)
    pairs = [(i, i + 1) for i in lower] + [(i + 1, i) for i in lower]
    return lax.ppermute(value, axis, pairs)


def scatter_sum(value, axes):
    count = lax.axis_size(axes)
    return lax.all_to_all(value.reshape(count, -1, LANES), axes, 0, 0).sum(0)


def gather(value, axes):
    return lax.all_to_all(jnp.broadcast_to(value[None], (lax.axis_size(axes),) + value.shape), axes, 0, 0)


def sum_everywhere(keep, send):
    value = keep + swap(send, "core", 0)
    value = scatter_sum(value, ("x", "y"))
    value = gather(value, "z").sum(0)
    value = gather(value, ("x", "y")).reshape(keep.shape)
    return value, swap(value, "core", 0)


def factor_panels(work, upper, inverse):
    size = work.shape[1]
    tiles = size // LANES
    lane = lanes_of((PANEL, LANES))
    sub = lax.broadcasted_iota(jnp.int32, (PANEL, LANES), 0)
    lane_row = lanes_of((1, LANES))
    for first in range(0, size, PANEL):
        home, at = first // LANES, first % LANES
        inside = (lane >= at) & (lane < at + PANEL)
        state = []
        for m in range(2):
            rows = [work[m, first : first + PANEL, t * LANES : (t + 1) * LANES] for t in range(tiles)]
            cols = [
                jnp.broadcast_to(rows[home][:, at + k : at + k + 1], (PANEL, LANES))
                for k in range(PANEL)
            ]
            block = jnp.where(inside, rows[home], 0.0)
            rows[home] = jnp.where(inside, jnp.where(lane == sub + at, 1.0, 0.0), rows[home])
            state.append((rows + [block], cols))
        for j in range(0, PANEL, 2):
            pair = (sub == j) | (sub == j + 1)
            for m in range(2):
                rows, cols = state[m]
                c0, c1 = cols[j], cols[j + 1]
                a, b, d = c0[j : j + 1], c1[j : j + 1], c1[j + 1 : j + 2]
                rdet = 1.0 / (a * d - b * b)
                i00, i01, i11 = d * rdet, -b * rdet, a * rdet
                m0 = c0 * i00 + c1 * i01
                m1 = c0 * i01 + c1 * i11
                m0 = jnp.where(sub == j, -i00, jnp.where(sub == j + 1, -i01, m0))
                m1 = jnp.where(sub == j, -i01, jnp.where(sub == j + 1, -i11, m1))
                for k in range(j + 2, PANEL):
                    ck = cols[k]
                    cols[k] = jnp.where(pair, 0.0, ck) - m0 * ck[j : j + 1] - m1 * ck[j + 1 : j + 2]
                ra = lax.rsqrt(a)
                ra = ra * (1.5 - 0.5 * a * ra * ra)
                ratio = b * ra * ra
                rest = d - ratio * b
                rb = lax.rsqrt(rest)
                rb = rb * (1.5 - 0.5 * rest * rb * rb)
                for t in range(tiles + 1):
                    r0, r1 = rows[t][j : j + 1], rows[t][j + 1 : j + 2]
                    done = (r0 * ra, (r1 - ratio * r0) * rb)
                    rows[t] = jnp.where(pair, 0.0, rows[t]) - m0 * r0 - m1 * r1
                    if t == tiles:
                        extra = done
                    elif t == home:
                        mine = done
                    else:
                        target, other = (inverse, upper) if t < home else (upper, inverse)
                        span = slice(t * LANES, (t + 1) * LANES)
                        target[m, first + j : first + j + 1, span] = done[0]
                        target[m, first + j + 1 : first + j + 2, span] = done[1]
                        other[m, first + j : first + j + 2, span] = jnp.zeros((2, LANES), jnp.float32)
                span = slice(home * LANES, (home + 1) * LANES)
                for e in range(2):
                    row = slice(first + j + e, first + j + e + 1)
                    left = lane_row < at + PANEL
                    inverse[m, row, span] = jnp.where(left, mine[e], 0.0)
                    corner = jnp.where(lane_row >= at + j + e, extra[e], 0.0)
                    upper[m, row, span] = jnp.where(left, corner, mine[e])
        for m in range(2):
            panel = jnp.concatenate(state[m][0][:tiles], axis=1)
            blocks = [panel]
            if at:
                blocks.insert(0, jnp.zeros((at, size), jnp.float32))
            if at + PANEL < LANES:
                blocks.append(jnp.zeros((LANES - at - PANEL, size), jnp.float32))
            panel = jnp.concatenate(blocks, axis=0)
            for start, stop in ((first + PANEL, first + 2 * PANEL), (first + 2 * PANEL, size)):
                if start >= min(stop, size):
                    continue
                left = work[m, start:stop, home * LANES : (home + 1) * LANES]
                change = high_dot(left, panel, ((1,), (0,)))
                place = lanes_of(left.shape)
                for t in range(tiles):
                    span = slice(t * LANES, (t + 1) * LANES)
                    if t == home:
                        old = jnp.where((place >= at) & (place < at + PANEL), 0.0, left)
                    else:
                        old = work[m, start:stop, span]
                    work[m, start:stop, span] = old - change[:, span]


def finish_kernel(
    scale, mine_ref, other_ref, adv_hbm, mean_ref, basis_hbm, root_hbm,
    pack_ref, work, upper, inverse, root, adv, basis, in_sem, out_sem, root_sem,
):
    lats, size, lons = adv.shape[0] - 1, adv.shape[1], adv.shape[2]
    steps = out_sem.shape[0]
    deep = lats // steps
    reads, writes = [], []
    for i in range(steps):
        span = pl.ds(i * deep, deep)
        reads.append(pltpu.make_async_copy(adv_hbm.at[span], adv.at[span], in_sem.at[i]))
        writes.append(pltpu.make_async_copy(basis.at[i], basis_hbm.at[:, span, :], out_sem.at[i]))
        reads[i].start()
    fore_ref = adv.at[lats, 0:lats]
    reads.append(pltpu.make_async_copy(adv_hbm.at[lats, 0:lats], fore_ref, in_sem.at[steps]))
    reads[steps].start()
    odd, half = odd_sides()[0], PACK // 2
    pack_ref[:half] = jnp.where(odd, other_ref[...], mine_ref[...])
    pack_ref[half:] = jnp.where(odd, mine_ref[...], other_ref[...])
    row = lax.broadcasted_iota(jnp.int32, (size, size), 0)
    col = lax.broadcasted_iota(jnp.int32, (size, size), 1)
    eye = row == col
    both = jnp.concatenate([pack_ref[0:size], pack_ref[size : 2 * size]], axis=1)
    turned = both.T
    line = lambda i: jnp.concatenate(
        [pack_ref[2 * size + i : 2 * size + i + 1], pack_ref[2 * size + i + 1 : 2 * size + i + 2]], axis=1
    )
    gram = jnp.where(row >= col, both, turned)
    obs_c = jnp.where(row < col, both, jnp.where(eye, line(0), turned))
    only = jnp.where(eye, both, 0.0)
    q_row = lax.rsqrt(jnp.sum(only, axis=0, keepdims=True))
    work[0] = gram * q_row * lax.rsqrt(jnp.sum(only, axis=1, keepdims=True))
    work[1] = jnp.where(eye, 1.0, 0.0) + obs_c / (size - 1.0)
    factor_panels(work, upper, inverse)
    finv = inverse[1]
    half = high_dot(jnp.broadcast_to(line(2), (8, size)), finv, ((1,), (1,)))
    coef = high_dot(half, finv, ((1,), (0,))) / (size - 1.0)
    left = jnp.concatenate([inverse[0] * (q_row * scale), coef], axis=0)
    reads[steps].wait()
    for i in range(steps):
        reads[i].wait()
        wide = jnp.concatenate([adv[i * deep + e] for e in range(deep)], axis=1)
        out = high_dot(left, wide, ((1,), (0,)))
        parts = [out[:, e * lons : (e + 1) * lons] for e in range(deep)]
        for r in range(0, size, 8):
            basis[i, r : r + 8] = jnp.swapaxes(jnp.stack([part[r : r + 8] for part in parts]), 0, 1)
        writes[i].start()
        for e, part in enumerate(parts):
            lat = i * deep + e
            mean_ref[lat : lat + 1] = fore_ref[lat : lat + 1] + part[size : size + 1]
    root[...] = high_dot(upper[0] * ((1.0 / q_row) / scale), finv, ((1,), (1,)))
    writes.append(pltpu.make_async_copy(root, root_hbm, root_sem))
    writes[-1].start()
    for copy in writes:
        copy.wait()


def finish(mine, other, advanced, scale):
    lats, size, lons = advanced.shape[0] - 1, advanced.shape[1], advanced.shape[2]
    steps = 4
    square = (size, size)
    return pl.pallas_call(
        functools.partial(finish_kernel, scale),
        in_specs=[VMEM, VMEM, HBM],
        out_specs=[VMEM, HBM, HBM],
        out_shape=[
            jax.ShapeDtypeStruct((lats, lons), jnp.float32),
            jax.ShapeDtypeStruct((size, lats, lons), jnp.float32),
            jax.ShapeDtypeStruct(square, jnp.float32),
        ],
        scratch_shapes=[pltpu.VMEM((PACK, lons), jnp.float32)]
        + [pltpu.VMEM((2,) + square, jnp.float32)] * 3
        + [
            pltpu.VMEM(square, jnp.float32),
            pltpu.VMEM((lats + 1, size, lons), jnp.float32),
            pltpu.VMEM((steps, size, lats // steps, lons), jnp.float32),
            pltpu.SemaphoreType.DMA((steps + 1,)),
            pltpu.SemaphoreType.DMA((steps,)),
            pltpu.SemaphoreType.DMA,
        ],
        compiler_params=room(50),
        name="finish",
    )(mine, other, advanced)


def body(mean_state, modes, east_vel, north_vel, sea_mask, obs_index, obs_value, obs_weight):
    count, lat_rows, lon_cols = modes.shape
    lat_one, lat_two, lon_one, lon_two = edges_of(modes, mean_state)
    band, tile = ("x", "core"), ("z", "y")
    sides = [swap(lat_one, band, 0), swap(lat_two, band, 1), swap(lon_one, tile, 0), swap(lon_two, tile, 1)]
    advanced, keep, send = sums_of(
        modes, mean_state, sides, east_vel, north_vel, sea_mask, obs_index, obs_value, obs_weight
    )
    mine, other = sum_everywhere(keep, send)
    points = lat_rows * lon_cols * lax.axis_size(band) * lax.axis_size(tile)
    mean_analysis, basis, root_factor = finish(mine, other, advanced, float(points) ** 0.5)
    return (mean_analysis, basis, root_factor)


def solution(mesh):
    mesh = Mesh(mesh.devices.reshape(4, 2, 8, 4), ("x", "core", "z", "y"))
    band, tile = ("x", "core"), ("z", "y")
    grid, blocks = P(band, tile), P(None, band, tile)
    obs = P(band, tile, None)
    return jax.shard_map(
        body,
        mesh=mesh,
        in_specs=(grid, blocks, grid, grid, grid, obs, obs, obs),
        out_specs=(grid, blocks, P()),
        check_vma=False,
    )
```

```python
import functools

import jax
import jax.numpy as jnp
from jax import lax
from jax.experimental import pallas as pl
from jax.experimental.pallas import tpu as pltpu
from jax.sharding import Mesh
from jax.sharding import PartitionSpec as P

HIGH = lax.Precision.HIGHEST
PANEL = 16
LANES = 128
PACK = 576
VMEM = pl.BlockSpec(memory_space=pltpu.VMEM)
HBM = pl.BlockSpec(memory_space=pltpu.HBM)


def room(mebibytes):
    return pltpu.CompilerParams(vmem_limit_bytes=mebibytes * 2**20)


def high_dot(a, b, dims):
    return lax.dot_general(
        a, b, (dims, ((), ())), precision=HIGH, preferred_element_type=jnp.float32
    )


def lanes_of(shape):
    return lax.broadcasted_iota(jnp.int32, shape, len(shape) - 1)


def by_latitude(block, first):
    count = block.shape[0]
    turned = [jnp.swapaxes(block[r : r + 8, first : first + 8, :], 0, 1) for r in range(0, count, 8)]
    return [jnp.concatenate([part[e] for part in turned], axis=0) for e in range(8)]


def reads_of(source, target, sems):
    rows = target.shape[1]
    copies = [
        pltpu.make_async_copy(source.at[pl.ds(i * rows, rows)], target.at[i], sems.at[i])
        for i in range(target.shape[0])
    ]
    for copy in copies:
        copy.start()
    return copies


def odd_sides():
    return lax.axis_index("core") == 1, lax.axis_index("y") % 2 == 1


def edges_kernel(
    modes_ref, mean_ref, lat_one, lat_two, lon_one, lon_two,
    low_ref, high_ref, west_ref, east_ref, block, in_sem, mean_sem,
):
    chunks, rows, lats, lons = block.shape
    groups = lons // lats
    total = chunks * rows
    packed = total // groups
    reads = reads_of(modes_ref, block, in_sem)
    means = [
        pltpu.make_async_copy(mean_ref, side.at[pl.ds(packed, lats)], mean_sem.at[i])
        for i, side in enumerate((west_ref, east_ref))
    ]
    for copy in means:
        copy.start()
    lane = lanes_of((rows, lons))
    for i in range(chunks):
        base = i * rows // packed * lats
        here = slice(i * rows % packed, i * rows % packed + rows)
        span = slice(i * rows, (i + 1) * rows)
        reads[i].wait()
        west = jnp.zeros((rows, lons), jnp.float32) if base == 0 else west_ref[here]
        east = jnp.zeros((rows, lons), jnp.float32) if base == 0 else east_ref[here]
        for first in range(0, lats, 8):
            for e, line in enumerate(by_latitude(block.at[i], first)):
                lat = first + e
                moved = pltpu.roll(line, (base + lat + 1) % lons, 1)
                west = jnp.where(lane == (base + lat + 1) % lons, moved, west)
                east = jnp.where(lane == base + lat, moved, east)
                if lat == 0:
                    low_ref[span] = line
                if lat == lats - 1:
                    high_ref[span] = line
        west_ref[here] = west
        east_ref[here] = east
    for copy in means:
        copy.wait()
    low_ref[total : total + 8] = jnp.broadcast_to(west_ref[packed : packed + 1], (8, lons))
    high_ref[total : total + 8] = jnp.broadcast_to(west_ref[packed + lats - 1 : packed + lats], (8, lons))
    odd_lat, odd_lon = odd_sides()
    for odd, below, above, one, two in (
        (odd_lat, low_ref, high_ref, lat_one, lat_two),
        (odd_lon, west_ref, east_ref, lon_one, lon_two),
    ):
        one[...] = jnp.where(odd, below[...], above[...])
        two[...] = jnp.where(odd, above[...], below[...])


def edges_of(modes, mean_state):
    count, lats, lons = modes.shape
    packed = count * lats // lons
    chunks = 8
    sides = [(count + 8, lons), (count + 8, lons), (packed + lats, lons), (packed + lats, lons)]
    return pl.pallas_call(
        edges_kernel,
        in_specs=[HBM] * 2,
        out_specs=[VMEM] * 4,
        out_shape=[jax.ShapeDtypeStruct(s, jnp.float32) for s in sides],
        scratch_shapes=[pltpu.VMEM(s, jnp.float32) for s in sides]
        + [
            pltpu.VMEM((chunks, count // chunks, lats, lons), jnp.float32),
            pltpu.SemaphoreType.DMA((chunks,)),
            pltpu.SemaphoreType.DMA((2,)),
        ],
        compiler_params=room(50),
        name="edges",
    )(modes, mean_state)


def slabs_kernel(modes_ref, slab_ref, block, in_sem):
    chunks, rows, lats, lons = block.shape
    for i, copy in enumerate(reads_of(modes_ref, block, in_sem)):
        copy.wait()
        for first in range(0, lats, 8):
            for e, line in enumerate(by_latitude(block.at[i], first)):
                slab_ref[first + e, i * rows : (i + 1) * rows, :] = line


def slabs_of(modes):
    count, lats, lons = modes.shape
    chunks = 8
    return pl.pallas_call(
        slabs_kernel,
        in_specs=[HBM],
        out_specs=VMEM,
        out_shape=jax.ShapeDtypeStruct((lats, count, lons), jnp.float32),
        scratch_shapes=[
            pltpu.VMEM((chunks, count // chunks, lats, lons), jnp.float32),
            pltpu.SemaphoreType.DMA((chunks,)),
        ],
        compiler_params=room(24),
        cost_estimate=pl.CostEstimate(flops=2**22, bytes_accessed=2 * modes.size * 4, transcendentals=0),
        name="slabs",
    )(modes)


def split(value):
    top = value.astype(jnp.bfloat16)
    return top, (value - top.astype(jnp.float32)).astype(jnp.bfloat16)


def pair_rows(a, b):
    return lax.dot_general(a, b, (((1,), (1,)), ((), ())), preferred_element_type=jnp.float32)


def sums_kernel(
    slab_ref, mean_ref, lat_one, lat_two, lon_one, lon_two, uvel_ref, vvel_ref, mask_ref,
    index_ref, value_ref, weight_ref, adv_hbm, keep_ref, send_ref,
    adv_ref, north_ref, south_ref, east_ref, west_ref, pack_ref, coef, parts, seen,
    out_sem,
):
    lats, count, lons = slab_ref.shape
    odd_lat, odd_lon = odd_sides()
    for odd, below, above, one, two in (
        (odd_lat, south_ref, north_ref, lat_one, lat_two),
        (odd_lon, west_ref, east_ref, lon_one, lon_two),
    ):
        above[...] = jnp.where(odd, two[...], one[...])
        below[...] = jnp.where(odd, one[...], two[...])
    chunks = out_sem.shape[0] - 1
    deep = lats // chunks
    writes = []
    for i in range(chunks):
        span = pl.ds(i * deep, deep)
        writes.append(pltpu.make_async_copy(adv_ref.at[span], adv_hbm.at[span], out_sem.at[i]))
    groups = lons // lats
    rows = count // groups
    sea = mask_ref[...].astype(jnp.float32)
    half_u, half_v = 0.5 * uvel_ref[...], 0.5 * vvel_ref[...]
    coef[0] = sea * 0.2
    coef[1] = sea * (0.2 - half_u)
    coef[2] = sea * (0.2 + half_u)
    coef[3] = sea * (0.2 - half_v)
    coef[4] = sea * (0.2 + half_v)
    first = lanes_of((lats, lons)) == 0
    last = lanes_of((lats, lons)) == lons - 1
    mean = mean_ref[...]
    eastern = jnp.where(last, east_ref[rows : rows + lats, 0:1], pltpu.roll(mean, lons - 1, 1))
    western = jnp.where(first, west_ref[rows : rows + lats, lons - 1 : lons], pltpu.roll(mean, 1, 1))
    northern = jnp.concatenate([mean[1:], north_ref[count : count + 1]], axis=0)
    southern = jnp.concatenate([south_ref[count : count + 1], mean[:-1]], axis=0)
    fore = coef[0] * mean + coef[1] * eastern + coef[2] * western
    fore_ref = adv_ref.at[lats, 0:lats]
    fore_ref[...] = fore + coef[3] * northern + coef[4] * southern
    writes.append(pltpu.make_async_copy(fore_ref, adv_hbm.at[lats, 0:lats], out_sem.at[chunks]))
    writes[-1].start()

    first = lanes_of((rows, lons)) == 0
    last = lanes_of((rows, lons)) == lons - 1

    def advance(lat, northern, southern):
        factors = [coef[i, pl.ds(lat, 1), :] for i in range(5)]
        out = []
        for g in range(groups):
            span = slice(g * rows, (g + 1) * rows)
            centre = slab_ref[lat, span, :]
            east_edge = pltpu.roll(east_ref[0:rows], (lons - 2 - g * lats - lat) % lons, 1)
            west_edge = pltpu.roll(west_ref[0:rows], (-g * lats - lat) % lons, 1)
            eastern = jnp.where(last, east_edge, pltpu.roll(centre, lons - 1, 1))
            western = jnp.where(first, west_edge, pltpu.roll(centre, 1, 1))
            moved = factors[0] * centre + factors[1] * eastern + factors[2] * western
            moved = moved + factors[3] * northern[span, :] + factors[4] * southern[span, :]
            adv_ref[lat, span, :] = moved
            out.append(moved)
        return jnp.concatenate(out, axis=0)

    observed = index_ref.shape[-1]
    point = index_ref[...]
    square = (observed, observed)
    eye = lax.broadcasted_iota(jnp.int32, square, 0) == lanes_of(square)
    point_col = jnp.sum(jnp.where(eye, point.astype(jnp.float32), 0.0), axis=1, keepdims=True)
    away = point_col.astype(jnp.int32) - lanes_of((observed, 2 * lons))

    parts[...] = jnp.zeros_like(parts)
    seen[...] = jnp.zeros_like(seen)
    for lat in range(0, lats, 2):
        rows_of = lambda i: south_ref if i < 0 else north_ref if i == lats else slab_ref.at[i]
        pair = [advance(i, rows_of(i + 1), rows_of(i - 1)) for i in (lat, lat + 1)]
        top, low = split(jnp.concatenate(pair, axis=1))
        parts[0] += pair_rows(top, top) + pair_rows(low, low)
        parts[1] += pair_rows(top, low)
        pick = jnp.where(away == lat * lons, 1.0, 0.0).astype(jnp.bfloat16)
        seen[...] += pair_rows(top, pick) + pair_rows(low, pick)
        if (lat + 2) % deep == 0:
            writes[lat // deep].start()

    lon_pick = jnp.where(lax.rem(point_col.astype(jnp.int32), lons) == lanes_of((observed, lons)), 1.0, 0.0)
    fore_at = high_dot(fore_ref[...], lon_pick, ((1,), (1,)))
    lat_of = lax.broadcasted_iota(jnp.int32, (lats, observed), 0)
    fore_at = jnp.sum(jnp.where(lat_of == point // lons, fore_at, 0.0), axis=0, keepdims=True)
    weights = weight_ref[...]
    diff = value_ref[...] - fore_at
    found = seen[...]
    obs_c = high_dot(found * weights, found, ((1,), (1,)))
    obs_b = high_dot(jnp.broadcast_to(weights * diff, (8, observed)), found, ((1,), (1,)))
    cross = parts[1]
    gram = parts[0] + (cross + cross.T)
    row = lax.broadcasted_iota(jnp.int32, (count, count), 0)
    col = lax.broadcasted_iota(jnp.int32, (count, count), 1)
    both = jnp.where(row >= col, gram, obs_c)
    diag_c = jnp.sum(jnp.where(row == col, obs_c, 0.0), axis=0, keepdims=True)
    pack_ref[0:count] = both[:, 0:lons]
    pack_ref[count : 2 * count] = both[:, lons:]
    pack_ref[2 * count :] = jnp.zeros((PACK - 2 * count, lons), jnp.float32)
    for i, line in enumerate((diag_c, obs_b[0:1])):
        pack_ref[2 * count + 2 * i : 2 * count + 2 * i + 1] = line[:, 0:lons]
        pack_ref[2 * count + 2 * i + 1 : 2 * count + 2 * i + 2] = line[:, lons:]
    half = PACK // 2
    keep_ref[...] = jnp.where(odd_lat, pack_ref[half:], pack_ref[:half])
    send_ref[...] = jnp.where(odd_lat, pack_ref[:half], pack_ref[half:])
    for copy in writes:
        copy.wait()


def sums_of(slabs, mean_state, sides, east_vel, north_vel, sea_mask, obs_index, obs_value, obs_weight):
    lats, count, lons = slabs.shape
    line = lambda x: x.reshape(1, -1)
    return pl.pallas_call(
        sums_kernel,
        in_specs=[VMEM] * 12,
        out_specs=[HBM] + [VMEM] * 2,
        out_shape=[jax.ShapeDtypeStruct((lats + 1, count, lons), jnp.float32)]
        + [jax.ShapeDtypeStruct((PACK // 2, lons), jnp.float32)] * 2,
        scratch_shapes=[
            pltpu.VMEM((lats + 1, count, lons), jnp.float32),
        ]
        + [pltpu.VMEM(side.shape, jnp.float32) for side in sides]
        + [
            pltpu.VMEM((PACK, lons), jnp.float32),
            pltpu.VMEM((5, lats, lons), jnp.float32),
            pltpu.VMEM((2, count, count), jnp.float32),
            pltpu.VMEM((count, obs_index.size), jnp.float32),
            pltpu.SemaphoreType.DMA((9,)),
        ],
        compiler_params=room(47),
        name="sums",
    )(slabs, mean_state, *sides, east_vel, north_vel, sea_mask, line(obs_index), line(obs_value), line(obs_weight))


def swap(value, axis, first):
    lower = range(first, lax.axis_size(axis) - 1, 2)
    pairs = [(i, i + 1) for i in lower] + [(i + 1, i) for i in lower]
    return lax.ppermute(value, axis, pairs)


def scatter_sum(value, axes):
    count = lax.axis_size(axes)
    return lax.all_to_all(value.reshape(count, -1, LANES), axes, 0, 0).sum(0)


def gather(value, axes):
    return lax.all_to_all(jnp.broadcast_to(value[None], (lax.axis_size(axes),) + value.shape), axes, 0, 0)


def sum_everywhere(keep, send):
    value = keep + swap(send, "core", 0)
    value = scatter_sum(value, ("x", "y"))
    value = gather(value, "z").sum(0)
    value = gather(value, ("x", "y")).reshape(keep.shape)
    return value, swap(value, "core", 0)


def factor_panels(work, upper, inverse):
    size = work.shape[1]
    tiles = size // LANES
    lane = lanes_of((PANEL, LANES))
    sub = lax.broadcasted_iota(jnp.int32, (PANEL, LANES), 0)
    lane_row = lanes_of((1, LANES))
    for first in range(0, size, PANEL):
        home, at = first // LANES, first % LANES
        inside = (lane >= at) & (lane < at + PANEL)
        state = []
        for m in range(2):
            rows = [work[m, first : first + PANEL, t * LANES : (t + 1) * LANES] for t in range(tiles)]
            cols = [
                jnp.broadcast_to(rows[home][:, at + k : at + k + 1], (PANEL, LANES))
                for k in range(PANEL)
            ]
            block = jnp.where(inside, rows[home], 0.0)
            rows[home] = jnp.where(inside, jnp.where(lane == sub + at, 1.0, 0.0), rows[home])
            state.append((rows + [block], cols))
        for j in range(0, PANEL, 2):
            pair = (sub == j) | (sub == j + 1)
            for m in range(2):
                rows, cols = state[m]
                c0, c1 = cols[j], cols[j + 1]
                a, b, d = c0[j : j + 1], c1[j : j + 1], c1[j + 1 : j + 2]
                rdet = 1.0 / (a * d - b * b)
                i00, i01, i11 = d * rdet, -b * rdet, a * rdet
                m0 = c0 * i00 + c1 * i01
                m1 = c0 * i01 + c1 * i11
                m0 = jnp.where(sub == j, -i00, jnp.where(sub == j + 1, -i01, m0))
                m1 = jnp.where(sub == j, -i01, jnp.where(sub == j + 1, -i11, m1))
                for k in range(j + 2, PANEL):
                    ck = cols[k]
                    cols[k] = jnp.where(pair, 0.0, ck) - m0 * ck[j : j + 1] - m1 * ck[j + 1 : j + 2]
                ra = lax.rsqrt(a)
                ra = ra * (1.5 - 0.5 * a * ra * ra)
                ratio = b * ra * ra
                rest = d - ratio * b
                rb = lax.rsqrt(rest)
                rb = rb * (1.5 - 0.5 * rest * rb * rb)
                for t in range(tiles + 1):
                    r0, r1 = rows[t][j : j + 1], rows[t][j + 1 : j + 2]
                    done = (r0 * ra, (r1 - ratio * r0) * rb)
                    rows[t] = jnp.where(pair, 0.0, rows[t]) - m0 * r0 - m1 * r1
                    if t == tiles:
                        extra = done
                    elif t == home:
                        mine = done
                    else:
                        target, other = (inverse, upper) if t < home else (upper, inverse)
                        span = slice(t * LANES, (t + 1) * LANES)
                        target[m, first + j : first + j + 1, span] = done[0]
                        target[m, first + j + 1 : first + j + 2, span] = done[1]
                        other[m, first + j : first + j + 2, span] = jnp.zeros((2, LANES), jnp.float32)
                span = slice(home * LANES, (home + 1) * LANES)
                for e in range(2):
                    row = slice(first + j + e, first + j + e + 1)
                    left = lane_row < at + PANEL
                    inverse[m, row, span] = jnp.where(left, mine[e], 0.0)
                    corner = jnp.where(lane_row >= at + j + e, extra[e], 0.0)
                    upper[m, row, span] = jnp.where(left, corner, mine[e])
        for m in range(2):
            panel = jnp.concatenate(state[m][0][:tiles], axis=1)
            blocks = [panel]
            if at:
                blocks.insert(0, jnp.zeros((at, size), jnp.float32))
            if at + PANEL < LANES:
                blocks.append(jnp.zeros((LANES - at - PANEL, size), jnp.float32))
            panel = jnp.concatenate(blocks, axis=0)
            for start, stop in ((first + PANEL, first + 2 * PANEL), (first + 2 * PANEL, size)):
                if start >= min(stop, size):
                    continue
                left = work[m, start:stop, home * LANES : (home + 1) * LANES]
                change = high_dot(left, panel, ((1,), (0,)))
                place = lanes_of(left.shape)
                for t in range(tiles):
                    span = slice(t * LANES, (t + 1) * LANES)
                    if t == home:
                        old = jnp.where((place >= at) & (place < at + PANEL), 0.0, left)
                    else:
                        old = work[m, start:stop, span]
                    work[m, start:stop, span] = old - change[:, span]


def finish_kernel(
    scale, mine_ref, other_ref, adv_hbm, mean_ref, basis_hbm, root_hbm,
    pack_ref, work, upper, inverse, root, adv, basis, in_sem, out_sem, root_sem,
):
    lats, size, lons = adv.shape[0] - 1, adv.shape[1], adv.shape[2]
    steps = out_sem.shape[0]
    deep = lats // steps
    reads, writes = [], []
    for i in range(steps):
        span = pl.ds(i * deep, deep)
        reads.append(pltpu.make_async_copy(adv_hbm.at[span], adv.at[span], in_sem.at[i]))
        writes.append(pltpu.make_async_copy(basis.at[i], basis_hbm.at[:, span, :], out_sem.at[i]))
        reads[i].start()
    fore_ref = adv.at[lats, 0:lats]
    reads.append(pltpu.make_async_copy(adv_hbm.at[lats, 0:lats], fore_ref, in_sem.at[steps]))
    reads[steps].start()
    odd, half = odd_sides()[0], PACK // 2
    pack_ref[:half] = jnp.where(odd, other_ref[...], mine_ref[...])
    pack_ref[half:] = jnp.where(odd, mine_ref[...], other_ref[...])
    row = lax.broadcasted_iota(jnp.int32, (size, size), 0)
    col = lax.broadcasted_iota(jnp.int32, (size, size), 1)
    eye = row == col
    both = jnp.concatenate([pack_ref[0:size], pack_ref[size : 2 * size]], axis=1)
    turned = both.T
    line = lambda i: jnp.concatenate(
        [pack_ref[2 * size + i : 2 * size + i + 1], pack_ref[2 * size + i + 1 : 2 * size + i + 2]], axis=1
    )
    gram = jnp.where(row >= col, both, turned)
    obs_c = jnp.where(row < col, both, jnp.where(eye, line(0), turned))
    only = jnp.where(eye, both, 0.0)
    q_row = lax.rsqrt(jnp.sum(only, axis=0, keepdims=True))
    work[0] = gram * q_row * lax.rsqrt(jnp.sum(only, axis=1, keepdims=True))
    work[1] = jnp.where(eye, 1.0, 0.0) + obs_c / (size - 1.0)
    factor_panels(work, upper, inverse)
    finv = inverse[1]
    half = high_dot(jnp.broadcast_to(line(2), (8, size)), finv, ((1,), (1,)))
    coef = high_dot(half, finv, ((1,), (0,))) / (size - 1.0)
    left = jnp.concatenate([inverse[0] * (q_row * scale), coef], axis=0)
    reads[steps].wait()
    for i in range(steps):
        reads[i].wait()
        wide = jnp.concatenate([adv[i * deep + e] for e in range(deep)], axis=1)
        out = high_dot(left, wide, ((1,), (0,)))
        parts = [out[:, e * lons : (e + 1) * lons] for e in range(deep)]
        for r in range(0, size, 8):
            basis[i, r : r + 8] = jnp.swapaxes(jnp.stack([part[r : r + 8] for part in parts]), 0, 1)
        writes[i].start()
        for e, part in enumerate(parts):
            lat = i * deep + e
            mean_ref[lat : lat + 1] = fore_ref[lat : lat + 1] + part[size : size + 1]
    root[...] = high_dot(upper[0] * ((1.0 / q_row) / scale), finv, ((1,), (1,)))
    writes.append(pltpu.make_async_copy(root, root_hbm, root_sem))
    writes[-1].start()
    for copy in writes:
        copy.wait()


def finish(mine, other, advanced, scale):
    lats, size, lons = advanced.shape[0] - 1, advanced.shape[1], advanced.shape[2]
    steps = 4
    square = (size, size)
    return pl.pallas_call(
        functools.partial(finish_kernel, scale),
        in_specs=[VMEM, VMEM, HBM],
        out_specs=[VMEM, HBM, HBM],
        out_shape=[
            jax.ShapeDtypeStruct((lats, lons), jnp.float32),
            jax.ShapeDtypeStruct((size, lats, lons), jnp.float32),
            jax.ShapeDtypeStruct(square, jnp.float32),
        ],
        scratch_shapes=[pltpu.VMEM((PACK, lons), jnp.float32)]
        + [pltpu.VMEM((2,) + square, jnp.float32)] * 3
        + [
            pltpu.VMEM(square, jnp.float32),
            pltpu.VMEM((lats + 1, size, lons), jnp.float32),
            pltpu.VMEM((steps, size, lats // steps, lons), jnp.float32),
            pltpu.SemaphoreType.DMA((steps + 1,)),
            pltpu.SemaphoreType.DMA((steps,)),
            pltpu.SemaphoreType.DMA,
        ],
        compiler_params=room(50),
        name="finish",
    )(mine, other, advanced)


def body(mean_state, modes, east_vel, north_vel, sea_mask, obs_index, obs_value, obs_weight):
    count, lat_rows, lon_cols = modes.shape
    lat_one, lat_two, lon_one, lon_two = edges_of(modes, mean_state)
    band, tile = ("x", "core"), ("z", "y")
    sides = [swap(lat_one, band, 0), swap(lat_two, band, 1), swap(lon_one, tile, 0), swap(lon_two, tile, 1)]
    advanced, keep, send = sums_of(
        slabs_of(modes), mean_state, sides, east_vel, north_vel, sea_mask, obs_index, obs_value, obs_weight
    )
    mine, other = sum_everywhere(keep, send)
    points = lat_rows * lon_cols * lax.axis_size(band) * lax.axis_size(tile)
    mean_analysis, basis, root_factor = finish(mine, other, advanced, float(points) ** 0.5)
    return (mean_analysis, basis, root_factor)


def solution(mesh):
    mesh = Mesh(mesh.devices.reshape(4, 2, 8, 4), ("x", "core", "z", "y"))
    band, tile = ("x", "core"), ("z", "y")
    grid, blocks = P(band, tile), P(None, band, tile)
    obs = P(band, tile, None)
    return jax.shard_map(
        body,
        mesh=mesh,
        in_specs=(grid, blocks, grid, grid, grid, obs, obs, obs),
        out_specs=(grid, blocks, P()),
        check_vma=False,
    )
```
